768 devices in a mesh: grid: 12 (over x, z_hi), state: 64 (over z_lo, y, core).
Axes of the slice: x: 4, y: 8, z: 12 (z_hi: 3, z_lo: 4; z = z_hi * 4 + z_lo), core: 2. Of those that a mesh axis runs over, the one named last changes fastest.
Arguments:
- orbitals: bfloat16 [512, 72, 16, 32], P('state', 'grid'), may hold values from -6 to 6
- potential: float32 [72, 16, 32], P('grid'), may hold values from -1.5 to 0.5
- occupation: float32 [512], P('state'), may hold values from 0.1 to 2
Outputs:
- subspace_energy: float32 [512, 512], P('state')
- subspace_gram: float32 [512, 512], P('state')
- density: float32 [72, 16, 32], P('grid')
The draws below stay inside these ranges and needn't reach their ends.
All inputs are finite; a program needn't handle non-finite values.
Results may differ from the reference program's by a relative error of at most 0.0021.
Values may be sent and summed in bfloat16 or wider, within the bound.
No kernel may reach another device: no remote copies, remote signals or barrier semaphores. Data moves between devices by JAX's collectives and lax.ppermute only.
A program may use at most 32 MiB of HBM per device.

```python
import math
import jax
import jax.numpy as jnp
from jax import lax

NS = 512
RADIUS = 6
DEGREE = 4
NX = 16
NY = 32
NZ = 72


def block_levels(stream_key, extent, split, least, top_value):
    gain, own = 1.0, jax.random.fold_in(stream_key, 6)
    for position, parts in split:
        draws = jnp.exp(jax.random.uniform(jax.random.fold_in(own, position), (parts,), jnp.float32, least / len(split), top_value / len(split)))
        gain = gain * jnp.repeat(draws, extent[position] // parts).reshape([-1 if axis == position else 1 for axis in range(len(extent))])
    return gain


def gaussian(rng, shape, width, most, pieces=(), kind=jnp.bfloat16):
    result = jax.random.normal(rng, shape, jnp.float32) * width
    if len(pieces) > 0:
        result = block_levels(rng, shape, pieces, -0.22, 0.18) * result
    return jnp.clip(result, min=-most, max=most).astype(kind)


def setup_inputs(seed: int = 0) -> dict:
    seeds = jax.random.split(jax.random.key(seed), 4)
    return {
        "orbitals": gaussian(seeds[0], (NS, NZ, NX, NY), 1.0, 6.0, ((0, 64), (1, 12))),
        "potential": jnp.clip(-1.5 + 2.0 * jax.random.uniform(seeds[1], (NZ, NX, NY), jnp.float32) ** block_levels(seeds[1], (NZ, NX, NY), ((0, 12),), -0.2, 0.2), -1.5, 0.5),
        "occupation": jnp.clip(jnp.exp(math.log(2.0) - 2.9957323 * jax.random.uniform(seeds[2], (NS,), jnp.float32) ** block_levels(seeds[2], (NS,), ((0, 64),), -0.2, 0.2)), 0.1, 2.0),
    }


stencil_weights = (-5369.0 / 1800.0, 12.0 / 7.0, -15.0 / 56.0, 10.0 / 189.0, -1.0 / 112.0, 2.0 / 1925.0, -1.0 / 16632.0)
cut_low = 1.0
cut_high = 12.0


def hamiltonian(slab_block, potential):
    values = slab_block.astype(jnp.float32)
    laplace = 3.0 * stencil_weights[0] * values
    for reach in range(1, RADIUS + 1):
        nearby = jnp.roll(values, reach, 1) + jnp.roll(values, -reach, 1)
        for dimension in (2, 3):
            nearby = nearby + jnp.roll(values, reach, dimension) + jnp.roll(values, -reach, dimension)
        laplace = laplace + stencil_weights[reach] * nearby
    return -0.5 * laplace + potential[None] * values


def reference(orbitals, potential, occupation):
    centre = 0.5 * (cut_high + cut_low)
    spread = 0.5 * (cut_high - cut_low)

    def scaled(slab_block):
        return (hamiltonian(slab_block, potential) - centre * slab_block.astype(jnp.float32)) / spread

    previous = orbitals
    current = scaled(orbitals).astype(jnp.bfloat16)
    for degree_index in range(1, DEGREE):
        following = (2.0 * scaled(current) - previous.astype(jnp.float32)).astype(jnp.bfloat16)
        previous = current
        current = following
    applied = hamiltonian(current, potential).astype(jnp.bfloat16)
    flat_orbit = current.reshape(NS, -1)
    flat_applied = applied.reshape(NS, -1)
    inverse_cells = 1.0 / (NZ * NX * NY)
    dims = (((1,), (1,)), ((), ()))
    energy = lax.dot_general(flat_applied, flat_orbit, dims, preferred_element_type=jnp.float32) * inverse_cells
    gram = lax.dot_general(flat_orbit, flat_orbit, dims, preferred_element_type=jnp.float32) * inverse_cells
    squares = jnp.square(current.astype(jnp.float32))
    density = jnp.sum(occupation[:, None, None, None] * squares, axis=0) / NS
    return (energy, gram, density)
```

```python
import jax
import jax.numpy as jnp
import numpy as np
from jax import lax
from jax.experimental import pallas as pl
from jax.experimental.pallas import tpu as pltpu
from jax.sharding import Mesh
from jax.sharding import PartitionSpec as P

NS = 512
RADIUS = 6
DEGREE = 4
NX = 16
NY = 32
NZ = 72
PLANE = NX * NY
SLABS = 12
THICK = NZ // SLABS

stencil_weights = (
    -5369.0 / 1800.0,
    12.0 / 7.0,
    -15.0 / 56.0,
    10.0 / 189.0,
    -1.0 / 112.0,
    2.0 / 1925.0,
    -1.0 / 16632.0,
)
cut_low = 1.0
cut_high = 12.0
centre = 0.5 * (cut_high + cut_low)
spread = 0.5 * (cut_high - cut_low)
bf16 = jnp.bfloat16
f32 = jnp.float32


def ring(count):
    line = np.zeros((count, count))
    rows = np.arange(count)
    for reach in range(1, RADIUS + 1):
        line[rows, (rows + reach) % count] += -0.5 * stencil_weights[reach]
        line[rows, (rows - reach) % count] += -0.5 * stencil_weights[reach]
    return line


def halves(matrix):
    high = matrix.astype(np.float32).astype(bf16)
    low = (matrix - high.astype(np.float64)).astype(np.float32).astype(bf16)
    return high, low


plane_high, plane_low = halves(
    np.kron(ring(NX), np.eye(NY)) + np.kron(np.eye(NX), ring(NY))
)
depth_high, depth_low = halves(np.kron(np.eye(2), ring(NZ)))


def unpacking():
    matrix = np.zeros((4 * NZ, 4 * NZ), np.float32)
    for slab in range(SLABS):
        for plane in range(THICK):
            for state in range(2):
                z = slab * THICK + plane
                base = slab * 4 * THICK + plane
                matrix[state * NZ + z, base + state * THICK] = 1.0
                matrix[(2 + state) * NZ + z, base + 2 * THICK] = 1.0
                matrix[(2 + state) * NZ + z, base + 3 * THICK] = 1.0
    return matrix.astype(bf16)


unpack = unpacking()


def product(a, b):
    return lax.dot_general(a, b, (((1,), (0,)), ((), ())), preferred_element_type=f32)


def filter_kernel(place, occupied, slabs, unpack_rows, high_xy, low_xy, high_z, low_z, out):
    count = 2 * NZ
    everything = product(unpack_rows[...], slabs[...])
    first = everything[:count]
    diagonal = everything[count:] - 1.5 * stencil_weights[0]
    shifted = diagonal - centre

    def hop(v):
        return (
            product(v, high_xy[...])
            + product(v, low_xy[...])
            + product(high_z[...], v)
            + product(low_z[...], v)
        )

    previous = first
    current = ((hop(first.astype(bf16)) + shifted * first) * (1.0 / spread)).astype(bf16)
    for _ in range(1, DEGREE):
        wide = current.astype(f32)
        following = (hop(current) + shifted * wide) * (2.0 / spread) - previous
        previous = wide
        current = following.astype(bf16)
    applied = (hop(current) + diagonal * current.astype(f32)).astype(bf16)

    row = lax.broadcasted_iota(jnp.int32, (48, count), 0)
    col = lax.broadcasted_iota(jnp.int32, (48, count), 1)
    group = (row >> 1) & 7
    z = THICK * (3 * (group >> 1) + place[1]) + 3 * (group & 1) + (row >> 4)
    pick = jnp.where(col == (row & 1) * NZ + z, 1.0, 0.0).astype(bf16)
    filtered_rows = product(pick, current).astype(bf16)
    applied_rows = product(pick, applied).astype(bf16)
    for lane_block in range(4):
        lanes = slice(lane_block * 128, lane_block * 128 + 128)
        for p in range(3):
            rows = slice(p * 16, p * 16 + 16)
            target = slice(lane_block * 16, lane_block * 16 + 16)
            out[target, p * 128 : p * 128 + 128] = filtered_rows[rows, lanes]
            out[target, 512 + p * 128 : 640 + p * 128] = applied_rows[rows, lanes]
    state = lax.broadcasted_iota(jnp.int32, (64, 128), 0) & 1
    lane = lax.broadcasted_iota(jnp.int32, (64, 128), 1)
    block = jnp.zeros((64, 128), f32)
    for piece in range(3):
        for k in range(2):
            value = occupied[piece * 8 + 2 * place[0] + k]
            block = jnp.where((lane == piece) & (state == k), value, block)
    out[:, 384:512] = block.astype(bf16)


def tile_kernel(own, gathered, out):
    row = lax.broadcasted_iota(jnp.int32, (NS, NS), 0)
    col = lax.broadcasted_iota(jnp.int32, (NS, NS), 1)
    source = ((((row >> 3) & 1) * 4 + ((row >> 1) & 3)) * 32 + (row >> 4)) * 2 + (row & 1)
    order = jnp.where(col == source, 1.0, 0.0).astype(bf16)
    ordered = product(order, gathered[...])
    states = ordered[:, :384]
    occupied = ordered[:, 384:385] + ordered[:, 385:386] + ordered[:, 386:387]
    density = jnp.sum(occupied * (states * states), axis=0, keepdims=True) * (1.0 / NS)

    row = lax.broadcasted_iota(jnp.int32, (128, 128), 0)
    col = lax.broadcasted_iota(jnp.int32, (128, 128), 1)
    source = ((row >> 1) & 1) * 64 + (row >> 2) * 2 + (row & 1)
    interleave = jnp.where(col == source, 1.0, 0.0).astype(bf16)
    stacked = jnp.concatenate([own[:, 512:896], own[:, 0:384]], axis=0)
    left = product(interleave, stacked).astype(bf16)
    out[:, 0:512] = lax.dot_general(
        left, states.astype(bf16), (((1,), (1,)), ((), ())), preferred_element_type=f32
    )
    kind = row & 3
    block = jnp.zeros((128, 128), f32)
    for p in range(3):
        block = jnp.where(kind == p, density[:, p * 128 : p * 128 + 128], block)
    out[:, 512:640] = block


def exchange(array, axes):
    return lax.all_to_all(array, axes, 0, 0, tiled=True)


def body(orbitals, potential, occupation):
    x = lax.axis_index("x")
    place = jnp.stack([x, lax.axis_index("zh")]).astype(jnp.int32)

    high = lax.reduce_precision(potential, 8, 7)
    low = potential - high
    wells = jnp.stack([high.astype(bf16), low.astype(bf16)]).reshape(1, 2 * THICK, PLANE)
    slabs = jnp.concatenate(
        [orbitals.reshape(4, 2 * THICK, PLANE), jnp.broadcast_to(wells, (4, 2 * THICK, PLANE))],
        axis=1,
    )
    slabs = jnp.broadcast_to(slabs[:, None], (4, 3, 4 * THICK, PLANE)).reshape(SLABS, 4 * THICK, PLANE)
    slabs = exchange(slabs, ("x", "zh")).reshape(4 * NZ, PLANE)

    occ_high = lax.reduce_precision(occupation, 8, 7)
    occ_rest = occupation - occ_high
    occ_mid = lax.reduce_precision(occ_rest, 8, 7)
    occupied = jnp.concatenate([occ_high, occ_mid, occ_rest - occ_mid])

    smem = pl.BlockSpec(memory_space=pltpu.SMEM)
    vmem = pl.BlockSpec(memory_space=pltpu.VMEM)
    params = pltpu.CompilerParams(vmem_limit_bytes=24 * 1024 * 1024)
    send = pl.pallas_call(
        filter_kernel,
        out_shape=jax.ShapeDtypeStruct((64, 896), bf16),
        in_specs=[smem, smem] + [vmem] * 6,
        out_specs=vmem,
        compiler_params=params,
        name="chebyshev",
    )(place, occupied, slabs, unpack, plane_high, plane_low, depth_high, depth_low)

    own = exchange(send.reshape(32, 2, 896), ("zl", "y")).reshape(64, 896)
    shared = jnp.broadcast_to(own[None, :, :512], (4, 64, 512))
    gathered = exchange(shared, "x").reshape(256, 512)
    gathered = lax.all_gather(gathered, "c", axis=0, tiled=True)

    partial = pl.pallas_call(
        tile_kernel,
        out_shape=jax.ShapeDtypeStruct((128, 640), f32),
        in_specs=[vmem] * 2,
        out_specs=vmem,
        compiler_params=params,
        name="tiles",
    )(own, gathered)

    parts = exchange(partial.reshape(32, 4, 640), ("zl", "y"))
    rows = jnp.sum(parts[:, :, :512], axis=0)
    cells = parts.reshape(4, 4, 2, 4, 640)[:, :, :, :3, 512:]
    cells = lax.dynamic_index_in_dim(cells, x, axis=1, keepdims=False)
    density = jnp.transpose(cells, (1, 2, 0, 3)).reshape(THICK, NX, NY)

    rows = exchange(jnp.broadcast_to(rows[None], (SLABS, 4, 512)), ("x", "zh"))
    rows = jnp.sum(rows.reshape(4, 3, 4, 512), axis=1) * (1.0 / (NZ * PLANE))
    return rows[:, :2].reshape(8, NS), rows[:, 2:].reshape(8, NS), density


def solution(mesh):
    fine = Mesh(mesh.devices.reshape(4, 3, 4, 8, 2), ("x", "zh", "zl", "y", "c"))
    grid, state = ("x", "zh"), ("zl", "y", "c")
    return jax.shard_map(
        body,
        mesh=fine,
        in_specs=(P(state, grid, None, None), P(grid, None, None), P(state)),
        out_specs=(P(state, None), P(state, None), P(grid, None, None)),
        check_vma=False,
    )
```

```python
import jax
import jax.numpy as jnp
import numpy as np
from jax import lax
from jax.experimental import pallas as pl
from jax.experimental.pallas import tpu as pltpu
from jax.sharding import Mesh
from jax.sharding import PartitionSpec as P

NS = 512
RADIUS = 6
DEGREE = 4
NX = 16
NY = 32
NZ = 72
PLANE = NX * NY
SLABS = 12
THICK = NZ // SLABS
CELLS = NZ * PLANE // 32
SHARED = CELLS + 128
PACKED = SHARED + CELLS

stencil_weights = (
    -5369.0 / 1800.0,
    12.0 / 7.0,
    -15.0 / 56.0,
    10.0 / 189.0,
    -1.0 / 112.0,
    2.0 / 1925.0,
    -1.0 / 16632.0,
)
cut_low = 1.0
cut_high = 12.0
centre = 0.5 * (cut_high + cut_low)
spread = 0.5 * (cut_high - cut_low)
bf16 = jnp.bfloat16
f32 = jnp.float32


def ring(count):
    line = np.zeros((count, count))
    rows = np.arange(count)
    for reach in range(1, RADIUS + 1):
        line[rows, (rows + reach) % count] += -0.5 * stencil_weights[reach]
        line[rows, (rows - reach) % count] += -0.5 * stencil_weights[reach]
    return line


def halves(matrix):
    high = matrix.astype(np.float32).astype(bf16)
    low = (matrix - high.astype(np.float64)).astype(np.float32).astype(bf16)
    return high, low


plane_high, plane_low = halves(
    np.kron(ring(NX), np.eye(NY)) + np.kron(np.eye(NX), ring(NY))
)

row_z = np.array(
    [
        THICK * (3 * (group >> 1) + hi) + 3 * (group & 1) + p
        for hi in range(3)
        for p in range(3)
        for group in range(8)
        for _ in range(2)
    ]
)
row_state = np.arange(2 * NZ) % 2
depth_high, depth_low = halves(
    ring(NZ)[row_z][:, row_z] * (row_state[:, None] == row_state[None, :])
)


def unpacking():
    matrix = np.zeros((4 * NZ, 4 * NZ), np.float32)
    rows = np.arange(2 * NZ)
    base = (row_z // THICK) * 4 * THICK + row_z % THICK
    matrix[rows, base + row_state * THICK] = 1.0
    matrix[2 * NZ + rows, base + 2 * THICK] = 1.0
    matrix[2 * NZ + rows, base + 3 * THICK] = 1.0
    return matrix.astype(bf16)


unpack = unpacking()


def product(a, b):
    return lax.dot_general(a, b, (((1,), (0,)), ((), ())), preferred_element_type=f32)


def filter_kernel(place, occupied, slabs, unpack_rows, high_xy, low_xy, high_z, low_z, out):
    count = 2 * NZ
    everything = product(unpack_rows[...], slabs[...])
    first = everything[:count]
    diagonal = everything[count:] - 1.5 * stencil_weights[0]
    shifted = diagonal - centre

    def hop(v):
        return (
            product(v, high_xy[...])
            + product(v, low_xy[...])
            + product(high_z[...], v)
            + product(low_z[...], v)
        )

    previous = first
    current = ((hop(first.astype(bf16)) + shifted * first) * (1.0 / spread)).astype(bf16)
    for _ in range(1, DEGREE):
        wide = current.astype(f32)
        following = (hop(current) + shifted * wide) * (2.0 / spread) - previous
        previous = wide
        current = following.astype(bf16)
    applied = (hop(current) + diagonal * current.astype(f32)).astype(bf16)

    for lane_block in range(4):
        lanes = slice(lane_block * 128, lane_block * 128 + 128)
        target = slice(lane_block * 16, lane_block * 16 + 16)
        for q in range(9):
            rows = slice(q * 16, q * 16 + 16)
            out[target, q * 128 : q * 128 + 128] = current[rows, lanes]
            out[target, SHARED + q * 128 : SHARED + q * 128 + 128] = applied[rows, lanes]
    state = lax.broadcasted_iota(jnp.int32, (64, 128), 0) & 1
    lane = lax.broadcasted_iota(jnp.int32, (64, 128), 1)
    block = jnp.zeros((64, 128), f32)
    for piece in range(3):
        for k in range(2):
            value = occupied[piece * 8 + 2 * place[0] + k]
            block = jnp.where((lane == piece) & (state == k), value, block)
    out[:, CELLS:SHARED] = block.astype(bf16)


def tile_kernel(place, own, mine, other, out):
    row = lax.broadcasted_iota(jnp.int32, (NS, NS), 0)
    col = lax.broadcasted_iota(jnp.int32, (NS, NS), 1)
    core = ((row >> 3) & 1) ^ place[2]
    source = ((core * 4 + ((row >> 1) & 3)) * 32 + (row >> 4)) * 2 + (row & 1)
    order = jnp.where(col == source, 1.0, 0.0).astype(bf16)
    gathered = jnp.concatenate([mine[...], other[...]], axis=0)
    ordered = product(order, gathered)
    states = ordered[:, :CELLS].astype(bf16)
    occupied = ordered[:, CELLS:SHARED]
    occupied = occupied[:, 0:1] + occupied[:, 1:2] + occupied[:, 2:3]
    third = CELLS // 3
    slab = jnp.where(place[1] == 0, ordered[:, :third], ordered[:, third : 2 * third])
    slab = jnp.where(place[1] == 2, ordered[:, 2 * third : CELLS], slab)
    density = jnp.sum(occupied * (slab * slab), axis=0, keepdims=True) * (1.0 / NS)

    row = lax.broadcasted_iota(jnp.int32, (128, 128), 0)
    col = lax.broadcasted_iota(jnp.int32, (128, 128), 1)
    source = ((row >> 1) & 1) * 64 + (row >> 2) * 2 + (row & 1)
    interleave = jnp.where(col == source, 1.0, 0.0).astype(bf16)
    stacked = jnp.concatenate([own[:, SHARED:PACKED], own[:, 0:CELLS]], axis=0)
    left = product(interleave, stacked).astype(bf16)
    out[:, 0:512] = lax.dot_general(
        left, states, (((1,), (1,)), ((), ())), preferred_element_type=f32
    )
    kind = row & 3
    block = jnp.zeros((128, 128), f32)
    for p in range(3):
        block = jnp.where(kind == p, density[:, p * 128 : p * 128 + 128], block)
    out[:, 512:640] = block


def exchange(array, axes):
    return lax.all_to_all(array, axes, 0, 0, tiled=True)


def body(orbitals, potential, occupation):
    x = lax.axis_index("x")
    place = jnp.stack([x, lax.axis_index("zh"), lax.axis_index("c")]).astype(jnp.int32)

    high = lax.reduce_precision(potential, 8, 7)
    low = potential - high
    wells = jnp.stack([high.astype(bf16), low.astype(bf16)]).reshape(1, 2 * THICK, PLANE)
    slabs = jnp.concatenate(
        [orbitals.reshape(4, 2 * THICK, PLANE), jnp.broadcast_to(wells, (4, 2 * THICK, PLANE))],
        axis=1,
    )
    slabs = jnp.broadcast_to(slabs[:, None], (4, 3, 4 * THICK, PLANE)).reshape(SLABS, 4 * THICK, PLANE)
    slabs = exchange(slabs, ("x", "zh")).reshape(4 * NZ, PLANE)

    occ_high = lax.reduce_precision(occupation, 8, 7)
    occ_rest = occupation - occ_high
    occ_mid = lax.reduce_precision(occ_rest, 8, 7)
    occupied = jnp.concatenate([occ_high, occ_mid, occ_rest - occ_mid])

    smem = pl.BlockSpec(memory_space=pltpu.SMEM)
    vmem = pl.BlockSpec(memory_space=pltpu.VMEM)
    params = pltpu.CompilerParams(vmem_limit_bytes=24 * 1024 * 1024)
    send = pl.pallas_call(
        filter_kernel,
        out_shape=jax.ShapeDtypeStruct((64, PACKED), bf16),
        in_specs=[smem, smem] + [vmem] * 6,
        out_specs=vmem,
        compiler_params=params,
        name="chebyshev",
    )(place, occupied, slabs, unpack, plane_high, plane_low, depth_high, depth_low)

    own = exchange(send.reshape(32, 2, PACKED), ("zl", "y")).reshape(64, PACKED)
    shared = jnp.broadcast_to(own[None, :, :SHARED], (4, 64, SHARED))
    mine = exchange(shared, "x").reshape(256, SHARED)
    other = lax.ppermute(mine, "c", [(0, 1), (1, 0)])

    partial = pl.pallas_call(
        tile_kernel,
        out_shape=jax.ShapeDtypeStruct((128, 640), f32),
        in_specs=[smem] + [vmem] * 3,
        out_specs=vmem,
        compiler_params=params,
        name="tiles",
    )(place, own, mine, other)

    parts = exchange(partial.reshape(32, 4, 640), ("zl", "y"))
    rows = jnp.sum(parts[:, :, :512], axis=0)
    cells = parts.reshape(4, 4, 2, 4, 640)[:, :, :, :3, 512:]
    cells = lax.dynamic_index_in_dim(cells, x, axis=1, keepdims=False)
    density = jnp.transpose(cells, (1, 2, 0, 3)).reshape(THICK, NX, NY)

    rows = exchange(jnp.broadcast_to(rows[None], (4, 4, 512)), "x") * (1.0 / (NZ * PLANE))
    return rows[:, :2].reshape(8, NS), rows[:, 2:].reshape(8, NS), density


def solution(mesh):
    fine = Mesh(mesh.devices.reshape(4, 3, 4, 8, 2), ("x", "zh", "zl", "y", "c"))
    grid, state = ("x", "zh"), ("zl", "y", "c")
    return jax.shard_map(
        body,
        mesh=fine,
        in_specs=(P(state, grid, None, None), P(grid, None, None), P(state)),
        out_specs=(P(state, None), P(state, None), P(grid, None, None)),
        check_vma=False,
    )
```

```python
import jax
import jax.numpy as jnp
import numpy as np
from jax import lax
from jax.experimental import pallas as pl
from jax.experimental.pallas import tpu as pltpu
from jax.sharding import Mesh
from jax.sharding import PartitionSpec as P

NS = 512
RADIUS = 6
DEGREE = 4
NX = 16
NY = 32
NZ = 72
PLANE = NX * NY
SLABS = 12
THICK = NZ // SLABS

stencil_weights = (
    -5369.0 / 1800.0,
    12.0 / 7.0,
    -15.0 / 56.0,
    10.0 / 189.0,
    -1.0 / 112.0,
    2.0 / 1925.0,
    -1.0 / 16632.0,
)
cut_low = 1.0
cut_high = 12.0
centre = 0.5 * (cut_high + cut_low)
spread = 0.5 * (cut_high - cut_low)
bf16 = jnp.bfloat16
f32 = jnp.float32


def ring(count):
    line = np.zeros((count, count))
    rows = np.arange(count)
    for reach in range(1, RADIUS + 1):
        line[rows, (rows + reach) % count] += -0.5 * stencil_weights[reach]
        line[rows, (rows - reach) % count] += -0.5 * stencil_weights[reach]
    return line


def halves(matrix):
    high = matrix.astype(np.float32).astype(bf16)
    low = (matrix - high.astype(np.float64)).astype(np.float32).astype(bf16)
    return high, low


plane_high, plane_low = halves(
    np.kron(ring(NX), np.eye(NY)) + np.kron(np.eye(NX), ring(NY))
)
depth_high, depth_low = halves(np.kron(np.eye(2), ring(NZ)))


def unpacking():
    matrix = np.zeros((4 * NZ, 4 * NZ), np.float32)
    for slab in range(SLABS):
        for plane in range(THICK):
            for state in range(2):
                z = slab * THICK + plane
                base = slab * 4 * THICK + plane
                matrix[state * NZ + z, base + state * THICK] = 1.0
                matrix[(2 + state) * NZ + z, base + 2 * THICK] = 1.0
                matrix[(2 + state) * NZ + z, base + 3 * THICK] = 1.0
    return matrix.astype(bf16)


unpack = unpacking()


def product(a, b):
    return lax.dot_general(a, b, (((1,), (0,)), ((), ())), preferred_element_type=f32)


def filter_kernel(occupation, slabs, unpack_rows, high_xy, low_xy, high_z, low_z, out):
    count = 2 * NZ
    everything = product(unpack_rows[...], slabs[...])
    first = everything[:count]
    diagonal = everything[count:] - 1.5 * stencil_weights[0]
    shifted = diagonal - centre

    def hop(v):
        return (
            product(v, high_xy[...])
            + product(v, low_xy[...])
            + product(high_z[...], v)
            + product(low_z[...], v)
        )

    previous = first
    current = ((hop(first.astype(bf16)) + shifted * first) * (1.0 / spread)).astype(bf16)
    for _ in range(1, DEGREE):
        wide = current.astype(f32)
        following = (hop(current) + shifted * wide) * (2.0 / spread) - previous
        previous = wide
        current = following.astype(bf16)
    applied = (hop(current) + diagonal * current.astype(f32)).astype(bf16)

    row = lax.broadcasted_iota(jnp.int32, (48, count), 0)
    col = lax.broadcasted_iota(jnp.int32, (48, count), 1)
    group = (row >> 1) & 7
    z = THICK * (3 * (group >> 1) + lax.axis_index("zh")) + 3 * (group & 1) + (row >> 4)
    pick = jnp.where(col == (row & 1) * NZ + z, 1.0, 0.0).astype(bf16)
    filtered_rows = product(pick, current).astype(bf16)
    applied_rows = product(pick, applied).astype(bf16)
    for lane_block in range(4):
        lanes = slice(lane_block * 128, lane_block * 128 + 128)
        for p in range(3):
            rows = slice(p * 16, p * 16 + 16)
            target = slice(lane_block * 16, lane_block * 16 + 16)
            out[target, p * 128 : p * 128 + 128] = filtered_rows[rows, lanes]
            out[target, 512 + p * 128 : 640 + p * 128] = applied_rows[rows, lanes]
    state = lax.broadcasted_iota(jnp.int32, (64, 128), 0) & 1
    lane = lax.broadcasted_iota(jnp.int32, (64, 128), 1)
    held = lax.broadcasted_iota(jnp.int32, (1, 8), 1)
    mine = 2 * lax.axis_index("x")
    block = jnp.zeros((64, 128), f32)
    for k in range(2):
        value = jnp.sum(jnp.where(held == mine + k, occupation[...], 0.0), axis=1, keepdims=True)
        for piece in range(3):
            part = value.astype(bf16).astype(f32)
            value = value - part
            block = jnp.where((lane == piece) & (state == k), part, block)
    out[:, 384:512] = block.astype(bf16)


def tile_kernel(own, gathered, out):
    row = lax.broadcasted_iota(jnp.int32, (NS, NS), 0)
    col = lax.broadcasted_iota(jnp.int32, (NS, NS), 1)
    source = ((((row >> 3) & 1) * 4 + ((row >> 1) & 3)) * 32 + (row >> 4)) * 2 + (row & 1)
    order = jnp.where(col == source, 1.0, 0.0).astype(bf16)
    ordered = product(order, gathered[...])
    states = ordered[:, :384]
    occupied = ordered[:, 384:385] + ordered[:, 385:386] + ordered[:, 386:387]
    density = jnp.sum(occupied * (states * states), axis=0, keepdims=True) * (1.0 / NS)

    row = lax.broadcasted_iota(jnp.int32, (128, 128), 0)
    col = lax.broadcasted_iota(jnp.int32, (128, 128), 1)
    source = ((row >> 1) & 1) * 64 + (row >> 2) * 2 + (row & 1)
    interleave = jnp.where(col == source, 1.0, 0.0).astype(bf16)
    stacked = jnp.concatenate([own[:, 512:896], own[:, 0:384]], axis=0)
    left = product(interleave, stacked).astype(bf16)
    tiles = lax.dot_general(
        left, states.astype(bf16), (((1,), (1,)), ((), ())), preferred_element_type=f32
    )
    out[:, 0:512] = tiles.astype(bf16)
    kind = row & 3
    block = jnp.zeros((128, 128), f32)
    for p in range(3):
        block = jnp.where(kind == p, density[:, p * 128 : p * 128 + 128], block)
    high = block.astype(bf16)
    out[:, 512:640] = high
    out[:, 640:768] = (block - high.astype(f32)).astype(bf16)


def sum_kernel(parts, rows, density):
    row = lax.broadcasted_iota(jnp.int32, (4 * SLABS, 128), 0)
    col = lax.broadcasted_iota(jnp.int32, (4 * SLABS, 128), 1)
    adder = jnp.where((row & 3) == (col & 3), 1.0, 0.0).astype(bf16)
    rows[...] = product(adder, parts[:, 0:512])
    row = lax.broadcasted_iota(jnp.int32, (8, 128), 0)
    col = lax.broadcasted_iota(jnp.int32, (8, 128), 1)
    half = jnp.where(row >= 3, 1, 0)
    for lane_block in range(4):
        sender = lane_block * 8 + 2 * lax.axis_index("x") + half
        pick = jnp.where((col == sender * 4 + row - 3 * half) & (row < THICK), 1.0, 0.0).astype(bf16)
        lanes = slice(lane_block * 128, lane_block * 128 + 128)
        density[:, lanes] = product(pick, parts[:, 512:640]) + product(pick, parts[:, 640:768])


def final_kernel(rows, cells, energy, gram, density):
    scale = 1.0 / (NZ * PLANE)
    for x in range(4):
        total = rows[12 * x : 12 * x + 4] + rows[12 * x + 4 : 12 * x + 8] + rows[12 * x + 8 : 12 * x + 12]
        total = total * scale
        energy[2 * x : 2 * x + 2] = total[0:2]
        gram[2 * x : 2 * x + 2] = total[2:4]
    for line in range(NX):
        density[:, line, :] = cells[0:THICK, line * NY : line * NY + NY]


def exchange(array, axes):
    return lax.all_to_all(array, axes, 0, 0, tiled=True)


def body(orbitals, potential, occupation):
    high = lax.reduce_precision(potential, 8, 7)
    low = potential - high
    wells = jnp.stack([high.astype(bf16), low.astype(bf16)]).reshape(1, 2 * THICK, PLANE)
    slabs = jnp.concatenate(
        [orbitals.reshape(4, 2 * THICK, PLANE), jnp.broadcast_to(wells, (4, 2 * THICK, PLANE))],
        axis=1,
    )
    slabs = jnp.broadcast_to(slabs[:, None], (4, 3, 4 * THICK, PLANE)).reshape(SLABS, 4 * THICK, PLANE)
    slabs = exchange(slabs, ("x", "zh")).reshape(4 * NZ, PLANE)

    vmem = pl.BlockSpec(memory_space=pltpu.VMEM)
    params = pltpu.CompilerParams(vmem_limit_bytes=24 * 1024 * 1024)
    send = pl.pallas_call(
        filter_kernel,
        out_shape=jax.ShapeDtypeStruct((64, 896), bf16),
        in_specs=[vmem] * 7,
        out_specs=vmem,
        compiler_params=params,
        name="chebyshev",
    )(occupation.reshape(1, 8), slabs, unpack, plane_high, plane_low, depth_high, depth_low)

    own = exchange(send.reshape(32, 2, 896), ("zl", "y")).reshape(64, 896)
    shared = jnp.broadcast_to(own[None, :, :512], (4, 64, 512))
    gathered = exchange(shared, "x").reshape(256, 512)
    gathered = lax.all_gather(gathered, "c", axis=0, tiled=True)

    partial = pl.pallas_call(
        tile_kernel,
        out_shape=jax.ShapeDtypeStruct((128, 768), bf16),
        in_specs=[vmem] * 2,
        out_specs=vmem,
        compiler_params=params,
        name="tiles",
    )(own, gathered)

    parts = exchange(partial.reshape(32, 4, 768), ("zl", "y")).reshape(128, 768)
    rows, cells = pl.pallas_call(
        sum_kernel,
        out_shape=[
            jax.ShapeDtypeStruct((4 * SLABS, NS), f32),
            jax.ShapeDtypeStruct((8, PLANE), f32),
        ],
        in_specs=[vmem],
        out_specs=[vmem] * 2,
        compiler_params=params,
        name="sums",
    )(parts)

    rows = exchange(rows.reshape(SLABS, 4, NS), ("x", "zh")).reshape(4 * SLABS, NS)
    return pl.pallas_call(
        final_kernel,
        out_shape=[
            jax.ShapeDtypeStruct((8, NS), f32),
            jax.ShapeDtypeStruct((8, NS), f32),
            jax.ShapeDtypeStruct((THICK, NX, NY), f32),
        ],
        in_specs=[vmem] * 2,
        out_specs=[vmem] * 3,
        compiler_params=params,
        name="results",
    )(rows, cells)


def solution(mesh):
    fine = Mesh(mesh.devices.reshape(4, 3, 4, 8, 2), ("x", "zh", "zl", "y", "c"))
    grid, state = ("x", "zh"), ("zl", "y", "c")
    return jax.shard_map(
        body,
        mesh=fine,
        in_specs=(P(state, grid, None, None), P(grid, None, None), P(state)),
        out_specs=(P(state, None), P(state, None), P(grid, None, None)),
        check_vma=False,
    )
```

```python
import jax
import jax.numpy as jnp
import numpy as np
from jax import lax
from jax.experimental import pallas as pl
from jax.experimental.pallas import tpu as pltpu
from jax.sharding import Mesh
from jax.sharding import PartitionSpec as P

NS = 512
RADIUS = 6
DEGREE = 4
NX = 16
NY = 32
NZ = 72
PLANE = NX * NY
SLABS = 12
THICK = NZ // SLABS

stencil_weights = (
    -5369.0 / 1800.0,
    12.0 / 7.0,
    -15.0 / 56.0,
    10.0 / 189.0,
    -1.0 / 112.0,
    2.0 / 1925.0,
    -1.0 / 16632.0,
)
cut_low = 1.0
cut_high = 12.0
centre = 0.5 * (cut_high + cut_low)
spread = 0.5 * (cut_high - cut_low)
bf16 = jnp.bfloat16
f32 = jnp.float32


def ring(count):
    line = np.zeros((count, count))
    rows = np.arange(count)
    for reach in range(1, RADIUS + 1):
        line[rows, (rows + reach) % count] += -0.5 * stencil_weights[reach]
        line[rows, (rows - reach) % count] += -0.5 * stencil_weights[reach]
    return line


def halves(matrix):
    high = matrix.astype(np.float32).astype(bf16)
    low = (matrix - high.astype(np.float64)).astype(np.float32).astype(bf16)
    return high, low


plane_high, plane_low = halves(
    np.kron(ring(NX), np.eye(NY)) + np.kron(np.eye(NX), ring(NY))
)
depth_high, depth_low = halves(np.kron(np.eye(2), ring(NZ)))


def unpacking():
    matrix = np.zeros((4 * NZ, 4 * NZ), np.float32)
    for slab in range(SLABS):
        for plane in range(THICK):
            for state in range(2):
                z = slab * THICK + plane
                base = slab * 4 * THICK + plane
                matrix[state * NZ + z, base + state * THICK] = 1.0
                matrix[(2 + state) * NZ + z, base + 2 * THICK] = 1.0
                matrix[(2 + state) * NZ + z, base + 3 * THICK] = 1.0
    return matrix.astype(bf16)


unpack = unpacking()


def product(a, b):
    return lax.dot_general(a, b, (((1,), (0,)), ((), ())), preferred_element_type=f32)


def filter_kernel(
    occupation, slabs, unpack_rows, high_xy, low_xy, high_z, low_z, out, occupied, arrived
):
    fetch = pltpu.make_async_copy(occupation, occupied, arrived)
    fetch.start()
    count = 2 * NZ
    everything = product(unpack_rows[...], slabs[...])
    first = everything[:count]
    diagonal = everything[count:] - 1.5 * stencil_weights[0]
    shifted = diagonal - centre

    def hop(v):
        return (
            product(v, high_xy[...])
            + product(v, low_xy[...])
            + product(high_z[...], v)
            + product(low_z[...], v)
        )

    previous = first
    current = ((hop(first.astype(bf16)) + shifted * first) * (1.0 / spread)).astype(bf16)
    for _ in range(1, DEGREE):
        wide = current.astype(f32)
        following = (hop(current) + shifted * wide) * (2.0 / spread) - previous
        previous = wide
        current = following.astype(bf16)
    applied = (hop(current) + diagonal * current.astype(f32)).astype(bf16)

    row = lax.broadcasted_iota(jnp.int32, (48, count), 0)
    col = lax.broadcasted_iota(jnp.int32, (48, count), 1)
    slab = 3 * ((row >> 1) & 3) + lax.axis_index("zh")
    z = THICK * slab + 3 * ((row >> 3) & 1) + (row >> 4)
    pick = jnp.where(col == (row & 1) * NZ + z, 1.0, 0.0).astype(bf16)
    filtered_rows = product(pick, current).astype(bf16)
    applied_rows = product(pick, applied).astype(bf16)
    for lane_block in range(4):
        lanes = slice(lane_block * 128, lane_block * 128 + 128)
        for p in range(3):
            rows = slice(p * 16, p * 16 + 16)
            target = slice(lane_block * 16, lane_block * 16 + 16)
            out[target, p * 128 : p * 128 + 128] = filtered_rows[rows, lanes]
            out[target, 512 + p * 128 : 640 + p * 128] = applied_rows[rows, lanes]
    state = lax.broadcasted_iota(jnp.int32, (64, 128), 0) & 1
    lane = lax.broadcasted_iota(jnp.int32, (64, 128), 1)
    held = lax.broadcasted_iota(jnp.int32, (1, 8), 1)
    mine = 2 * lax.axis_index("x")
    block = jnp.zeros((64, 128), f32)
    fetch.wait()
    for k in range(2):
        value = jnp.sum(jnp.where(held == mine + k, occupied[...], 0.0), axis=1, keepdims=True)
        for piece in range(3):
            part = value.astype(bf16).astype(f32)
            value = value - part
            block = jnp.where((lane == piece) & (state == k), part, block)
    out[:, 384:512] = block.astype(bf16)


def tile_kernel(own, gathered, out):
    row = lax.broadcasted_iota(jnp.int32, (NS, NS), 0)
    col = lax.broadcasted_iota(jnp.int32, (NS, NS), 1)
    source = (((row >> 3) & 1) * 4 + (row >> 7)) * 64 + ((row >> 4) & 7) * 8 + (row & 7)
    order = jnp.where(col == source, 1.0, 0.0).astype(bf16)
    ordered = product(order, gathered[...])
    states = ordered[:, :384]
    occupied = ordered[:, 384:385] + ordered[:, 385:386] + ordered[:, 386:387]
    density = jnp.sum(occupied * (states * states), axis=0, keepdims=True) * (1.0 / NS)

    row = lax.broadcasted_iota(jnp.int32, (128, 128), 0)
    col = lax.broadcasted_iota(jnp.int32, (128, 128), 1)
    source = ((row >> 3) & 1) * 64 + (row >> 4) * 8 + (row & 7)
    interleave = jnp.where(col == source, 1.0, 0.0).astype(bf16)
    stacked = jnp.concatenate([own[:, 512:896], own[:, 0:384]], axis=0)
    left = product(interleave, stacked).astype(bf16)
    tiles = lax.dot_general(
        left, states.astype(bf16), (((1,), (1,)), ((), ())), preferred_element_type=f32
    )
    out[:, 0:512] = tiles.astype(bf16)
    high = density.astype(bf16).astype(f32)
    kind = row & 15
    block = jnp.zeros((128, 128), f32)
    for p in range(3):
        lanes = slice(p * 128, p * 128 + 128)
        block = jnp.where(kind == p, high[:, lanes], block)
        block = jnp.where(kind == 3 + p, density[:, lanes] - high[:, lanes], block)
    out[:, 512:640] = block.astype(bf16)


def sum_kernel(parts, rows, density):
    row = lax.broadcasted_iota(jnp.int32, (16, 128), 0)
    col = lax.broadcasted_iota(jnp.int32, (16, 128), 1)
    adder = jnp.where(row == (col & 15), 1.0, 0.0).astype(bf16)
    total = product(adder, parts[:, 0:512]).astype(bf16)
    for receiver in range(SLABS):
        rows[receiver * 16 : receiver * 16 + 16] = total
    row = lax.broadcasted_iota(jnp.int32, (8, 128), 0)
    col = lax.broadcasted_iota(jnp.int32, (8, 128), 1)
    half = jnp.where(row >= 3, 1, 0)
    for lane_block in range(4):
        first = (lane_block * 2 + half) * 16 + row - 3 * half
        hit = ((col == first) | (col == first + 3)) & (row < THICK)
        pick = jnp.where(hit, 1.0, 0.0).astype(bf16)
        lanes = slice(lane_block * 128, lane_block * 128 + 128)
        density[:, lanes] = product(pick, parts[:, 512:640])


def final_kernel(rows, cells, energy, gram, density):
    total = rows[0:16].astype(f32)
    for sender in range(1, SLABS):
        total = total + rows[sender * 16 : sender * 16 + 16].astype(f32)
    total = total * (1.0 / (NZ * PLANE))
    energy[...] = total[0:8]
    gram[...] = total[8:16]
    for line in range(NX):
        density[:, line, :] = cells[0:THICK, line * NY : line * NY + NY]


def exchange(array, axes):
    return lax.all_to_all(array, axes, 0, 0, tiled=True)


def body(orbitals, potential, occupation):
    high = lax.reduce_precision(potential, 8, 7)
    low = potential - high
    wells = jnp.stack([high.astype(bf16), low.astype(bf16)]).reshape(1, 2 * THICK, PLANE)
    slabs = jnp.concatenate(
        [orbitals.reshape(4, 2 * THICK, PLANE), jnp.broadcast_to(wells, (4, 2 * THICK, PLANE))],
        axis=1,
    )
    slabs = jnp.broadcast_to(slabs[:, None], (4, 3, 4 * THICK, PLANE)).reshape(SLABS, 4 * THICK, PLANE)
    slabs = exchange(slabs, ("x", "zh")).reshape(4 * NZ, PLANE)

    vmem = pl.BlockSpec(memory_space=pltpu.VMEM)
    params = pltpu.CompilerParams(vmem_limit_bytes=24 * 1024 * 1024)
    send = pl.pallas_call(
        filter_kernel,
        out_shape=jax.ShapeDtypeStruct((64, 896), bf16),
        in_specs=[pl.BlockSpec(memory_space=pltpu.HBM)] + [vmem] * 6,
        out_specs=vmem,
        scratch_shapes=[pltpu.VMEM((1, 8), f32), pltpu.SemaphoreType.DMA(())],
        compiler_params=params,
        name="chebyshev",
    )(occupation.reshape(1, 8), slabs, unpack, plane_high, plane_low, depth_high, depth_low)

    own = exchange(send.reshape(32, 2, 896), ("y", "x")).reshape(64, 896)
    shared = jnp.broadcast_to(own[None, :, :512], (4, 64, 512))
    gathered = exchange(shared, "zl").reshape(256, 512)
    gathered = lax.all_gather(gathered, "c", axis=0, tiled=True)

    partial = pl.pallas_call(
        tile_kernel,
        out_shape=jax.ShapeDtypeStruct((128, 640), bf16),
        in_specs=[vmem] * 2,
        out_specs=vmem,
        compiler_params=params,
        name="tiles",
    )(own, gathered)

    parts = exchange(partial.reshape(8, 16, 640), "y").reshape(128, 640)
    rows, cells = pl.pallas_call(
        sum_kernel,
        out_shape=[
            jax.ShapeDtypeStruct((16 * SLABS, NS), bf16),
            jax.ShapeDtypeStruct((8, PLANE), f32),
        ],
        in_specs=[vmem],
        out_specs=[vmem] * 2,
        compiler_params=params,
        name="sums",
    )(parts)

    rows = exchange(rows.reshape(SLABS, 16, NS), ("x", "zh")).reshape(16 * SLABS, NS)
    return pl.pallas_call(
        final_kernel,
        out_shape=[
            jax.ShapeDtypeStruct((8, NS), f32),
            jax.ShapeDtypeStruct((8, NS), f32),
            jax.ShapeDtypeStruct((THICK, NX, NY), f32),
        ],
        in_specs=[vmem] * 2,
        out_specs=[vmem] * 3,
        compiler_params=params,
        name="results",
    )(rows, cells)


def solution(mesh):
    fine = Mesh(mesh.devices.reshape(4, 3, 4, 8, 2), ("x", "zh", "zl", "y", "c"))
    grid, state = ("x", "zh"), ("zl", "y", "c")
    return jax.shard_map(
        body,
        mesh=fine,
        in_specs=(P(state, grid, None, None), P(grid, None, None), P(state)),
        out_specs=(P(state, None), P(state, None), P(grid, None, None)),
        check_vma=False,
    )
```

```python
import jax
import jax.numpy as jnp
import numpy as np
from jax import lax
from jax.experimental import pallas as pl
from jax.experimental.pallas import tpu as pltpu
from jax.sharding import Mesh
from jax.sharding import PartitionSpec as P

NS = 512
RADIUS = 6
DEGREE = 4
NX = 16
NY = 32
NZ = 72
PLANE = NX * NY
SLABS = 12
THICK = NZ // SLABS

stencil_weights = (
    -5369.0 / 1800.0,
    12.0 / 7.0,
    -15.0 / 56.0,
    10.0 / 189.0,
    -1.0 / 112.0,
    2.0 / 1925.0,
    -1.0 / 16632.0,
)
cut_low = 1.0
cut_high = 12.0
centre = 0.5 * (cut_high + cut_low)
spread = 0.5 * (cut_high - cut_low)
bf16 = jnp.bfloat16
f32 = jnp.float32


def ring(count):
    line = np.zeros((count, count))
    rows = np.arange(count)
    for reach in range(1, RADIUS + 1):
        line[rows, (rows + reach) % count] += -0.5 * stencil_weights[reach]
        line[rows, (rows - reach) % count] += -0.5 * stencil_weights[reach]
    return line


def halves(matrix):
    high = matrix.astype(np.float32).astype(bf16)
    low = (matrix - high.astype(np.float64)).astype(np.float32).astype(bf16)
    return high, low


plane_high, plane_low = halves(
    np.kron(ring(NX), np.eye(NY)) + np.kron(np.eye(NX), ring(NY))
)
depth_high, depth_low = halves(np.kron(np.eye(2), ring(NZ)))


def unpacking():
    matrix = np.zeros((4 * NZ, 4 * NZ), np.float32)
    for slab in range(SLABS):
        for plane in range(THICK):
            for state in range(2):
                z = slab * THICK + plane
                base = slab * 4 * THICK + plane
                matrix[state * NZ + z, base + state * THICK] = 1.0
                matrix[(2 + state) * NZ + z, base + 2 * THICK] = 1.0
                matrix[(2 + state) * NZ + z, base + 3 * THICK] = 1.0
    return matrix.astype(bf16)


unpack = unpacking()


def product(a, b):
    return lax.dot_general(a, b, (((1,), (0,)), ((), ())), preferred_element_type=f32)


def filter_kernel(occupation, slabs, unpack_rows, high_xy, low_xy, high_z, low_z, out):
    count = 2 * NZ
    everything = product(unpack_rows[...], slabs[...])
    first = everything[:count]
    diagonal = everything[count:] - 1.5 * stencil_weights[0]
    shifted = diagonal - centre

    def hop(v):
        return (
            product(v, high_xy[...])
            + product(v, low_xy[...])
            + product(high_z[...], v)
            + product(low_z[...], v)
        )

    previous = first
    current = ((hop(first.astype(bf16)) + shifted * first) * (1.0 / spread)).astype(bf16)
    for _ in range(1, DEGREE):
        wide = current.astype(f32)
        following = (hop(current) + shifted * wide) * (2.0 / spread) - previous
        previous = wide
        current = following.astype(bf16)
    applied = (hop(current) + diagonal * current.astype(f32)).astype(bf16)

    row = lax.broadcasted_iota(jnp.int32, (48, count), 0)
    col = lax.broadcasted_iota(jnp.int32, (48, count), 1)
    group = (row >> 1) & 7
    z = THICK * (3 * (group >> 1) + lax.axis_index("zh")) + 3 * (group & 1) + (row >> 4)
    pick = jnp.where(col == (row & 1) * NZ + z, 1.0, 0.0).astype(bf16)
    filtered_rows = product(pick, current).astype(bf16)
    applied_rows = product(pick, applied).astype(bf16)
    for lane_block in range(4):
        lanes = slice(lane_block * 128, lane_block * 128 + 128)
        for p in range(3):
            rows = slice(p * 16, p * 16 + 16)
            target = slice(lane_block * 16, lane_block * 16 + 16)
            out[target, p * 128 : p * 128 + 128] = filtered_rows[rows, lanes]
            out[target, 512 + p * 128 : 640 + p * 128] = applied_rows[rows, lanes]
    state = lax.broadcasted_iota(jnp.int32, (64, 128), 0) & 1
    lane = lax.broadcasted_iota(jnp.int32, (64, 128), 1)
    held = lax.broadcasted_iota(jnp.int32, (1, 8), 1)
    mine = 2 * lax.axis_index("x")
    block = jnp.zeros((64, 128), f32)
    for k in range(2):
        value = jnp.sum(jnp.where(held == mine + k, occupation[...], 0.0), axis=1, keepdims=True)
        for piece in range(3):
            part = value.astype(bf16).astype(f32)
            value = value - part
            block = jnp.where((lane == piece) & (state == k), part, block)
    out[:, 384:512] = block.astype(bf16)


def tile_kernel(own, gathered, out):
    row = lax.broadcasted_iota(jnp.int32, (NS, NS), 0)
    col = lax.broadcasted_iota(jnp.int32, (NS, NS), 1)
    source = ((((row >> 3) & 1) * 4 + ((row >> 1) & 3)) * 32 + (row >> 4)) * 2 + (row & 1)
    order = jnp.where(col == source, 1.0, 0.0).astype(bf16)
    ordered = product(order, gathered[...])
    states = ordered[:, :384]
    occupied = ordered[:, 384:385] + ordered[:, 385:386] + ordered[:, 386:387]
    density = jnp.sum(occupied * (states * states), axis=0, keepdims=True) * (1.0 / NS)

    row = lax.broadcasted_iota(jnp.int32, (128, 128), 0)
    col = lax.broadcasted_iota(jnp.int32, (128, 128), 1)
    source = ((row >> 1) & 1) * 64 + (row >> 2) * 2 + (row & 1)
    interleave = jnp.where(col == source, 1.0, 0.0).astype(bf16)
    stacked = jnp.concatenate([own[:, 512:896], own[:, 0:384]], axis=0)
    left = product(interleave, stacked).astype(bf16)
    tiles = lax.dot_general(
        left, states.astype(bf16), (((1,), (1,)), ((), ())), preferred_element_type=f32
    )
    out[:, 0:512] = tiles.astype(bf16)
    kind = row & 3
    block = jnp.zeros((128, 128), f32)
    for p in range(3):
        block = jnp.where(kind == p, density[:, p * 128 : p * 128 + 128], block)
    high = block.astype(bf16)
    out[:, 512:640] = high
    out[:, 640:768] = (block - high.astype(f32)).astype(bf16)


def sum_kernel(parts, rows, density):
    row = lax.broadcasted_iota(jnp.int32, (4 * SLABS, 128), 0)
    col = lax.broadcasted_iota(jnp.int32, (4 * SLABS, 128), 1)
    adder = jnp.where((row & 3) == (col & 3), 1.0, 0.0).astype(bf16)
    rows[...] = product(adder, parts[:, 0:512]).astype(bf16)
    row = lax.broadcasted_iota(jnp.int32, (8, 128), 0)
    col = lax.broadcasted_iota(jnp.int32, (8, 128), 1)
    half = jnp.where(row >= 3, 1, 0)
    for lane_block in range(4):
        sender = lane_block * 8 + 2 * lax.axis_index("x") + half
        pick = jnp.where((col == sender * 4 + row - 3 * half) & (row < THICK), 1.0, 0.0).astype(bf16)
        lanes = slice(lane_block * 128, lane_block * 128 + 128)
        density[:, lanes] = product(pick, parts[:, 512:640]) + product(pick, parts[:, 640:768])


def final_kernel(received, cells, energy, gram, density):
    rows = received[...].astype(f32)
    scale = 1.0 / (NZ * PLANE)
    for x in range(4):
        total = rows[12 * x : 12 * x + 4] + rows[12 * x + 4 : 12 * x + 8] + rows[12 * x + 8 : 12 * x + 12]
        total = total * scale
        energy[2 * x : 2 * x + 2] = total[0:2]
        gram[2 * x : 2 * x + 2] = total[2:4]
    for line in range(NX):
        density[:, line, :] = cells[0:THICK, line * NY : line * NY + NY]


def exchange(array, axes):
    return lax.all_to_all(array, axes, 0, 0, tiled=True)


def body(orbitals, potential, occupation):
    high = lax.reduce_precision(potential, 8, 7)
    low = potential - high
    wells = jnp.stack([high.astype(bf16), low.astype(bf16)]).reshape(1, 2 * THICK, PLANE)
    slabs = jnp.concatenate(
        [orbitals.reshape(4, 2 * THICK, PLANE), jnp.broadcast_to(wells, (4, 2 * THICK, PLANE))],
        axis=1,
    )
    slabs = jnp.broadcast_to(slabs[:, None], (4, 3, 4 * THICK, PLANE)).reshape(SLABS, 4 * THICK, PLANE)
    slabs = exchange(slabs, ("x", "zh")).reshape(4 * NZ, PLANE)

    vmem = pl.BlockSpec(memory_space=pltpu.VMEM)
    params = pltpu.CompilerParams(vmem_limit_bytes=24 * 1024 * 1024)
    send = pl.pallas_call(
        filter_kernel,
        out_shape=jax.ShapeDtypeStruct((64, 896), bf16),
        in_specs=[vmem] * 7,
        out_specs=vmem,
        compiler_params=params,
        name="chebyshev",
    )(occupation.reshape(1, 8), slabs, unpack, plane_high, plane_low, depth_high, depth_low)

    own = exchange(send.reshape(32, 2, 896), ("zl", "y")).reshape(64, 896)
    shared = jnp.broadcast_to(own[None, :, :512], (4, 64, 512))
    gathered = exchange(shared, "x").reshape(256, 512)
    gathered = lax.all_gather(gathered, "c", axis=0, tiled=True)

    partial = pl.pallas_call(
        tile_kernel,
        out_shape=jax.ShapeDtypeStruct((128, 768), bf16),
        in_specs=[vmem] * 2,
        out_specs=vmem,
        compiler_params=params,
        name="tiles",
    )(own, gathered)

    parts = exchange(partial.reshape(32, 4, 768), ("zl", "y")).reshape(128, 768)
    rows, cells = pl.pallas_call(
        sum_kernel,
        out_shape=[
            jax.ShapeDtypeStruct((4 * SLABS, NS), bf16),
            jax.ShapeDtypeStruct((8, PLANE), f32),
        ],
        in_specs=[vmem],
        out_specs=[vmem] * 2,
        compiler_params=params,
        name="sums",
    )(parts)

    rows = exchange(rows.reshape(SLABS, 4, NS), ("x", "zh")).reshape(4 * SLABS, NS)
    return pl.pallas_call(
        final_kernel,
        out_shape=[
            jax.ShapeDtypeStruct((8, NS), f32),
            jax.ShapeDtypeStruct((8, NS), f32),
            jax.ShapeDtypeStruct((THICK, NX, NY), f32),
        ],
        in_specs=[vmem] * 2,
        out_specs=[vmem] * 3,
        compiler_params=params,
        name="results",
    )(rows, cells)


def solution(mesh):
    fine = Mesh(mesh.devices.reshape(4, 3, 4, 8, 2), ("x", "zh", "zl", "y", "c"))
    grid, state = ("x", "zh"), ("zl", "y", "c")
    return jax.shard_map(
        body,
        mesh=fine,
        in_specs=(P(state, grid, None, None), P(grid, None, None), P(state)),
        out_specs=(P(state, None), P(state, None), P(grid, None, None)),
        check_vma=False,
    )
```

```python
import math

import jax
import jax.numpy as jnp
import numpy as np
from jax import lax
from jax.experimental import pallas as pl
from jax.experimental.pallas import tpu as pltpu
from jax.sharding import Mesh
from jax.sharding import PartitionSpec as P

NS = 512
RADIUS = 6
DEGREE = 4
NX = 16
NY = 32
NZ = 72
PLANE = NX * NY
SLABS = 12
THICK = NZ // SLABS

stencil_weights = (
    -5369.0 / 1800.0,
    12.0 / 7.0,
    -15.0 / 56.0,
    10.0 / 189.0,
    -1.0 / 112.0,
    2.0 / 1925.0,
    -1.0 / 16632.0,
)
cut_low = 1.0
cut_high = 12.0
centre = 0.5 * (cut_high + cut_low)
spread = 0.5 * (cut_high - cut_low)
CODE = 120.0
OFFSET = 0.5
bf16 = jnp.bfloat16
f32 = jnp.float32


def ring(count):
    line = np.zeros((count, count))
    rows = np.arange(count)
    for reach in range(1, RADIUS + 1):
        line[rows, (rows + reach) % count] += -0.5 * stencil_weights[reach]
        line[rows, (rows - reach) % count] += -0.5 * stencil_weights[reach]
    return line


def halves(matrix):
    high = matrix.astype(np.float32).astype(bf16)
    low = (matrix - high.astype(np.float64)).astype(np.float32).astype(bf16)
    return high, low


plane_high, plane_low = halves(
    np.kron(ring(NX), np.eye(NY)) + np.kron(np.eye(NX), ring(NY))
)
depth_high, depth_low = halves(np.kron(np.eye(2), ring(NZ)))


def unpacking():
    matrix = np.zeros((9 * NZ, SLABS * 8), np.float32)
    for slab in range(SLABS):
        for plane in range(THICK):
            z = slab * THICK + plane
            for state in range(2):
                line = state * THICK + plane
                start = 0 if line < 8 else 6 * NZ
                matrix[start + state * NZ + z, slab * 8 + line % 8] = 1.0
            if plane < 4:
                matrix[8 * NZ + z, slab * 8 + 4 + plane] = 1.0
            else:
                for block in range(4):
                    matrix[(2 + block) * NZ + z, slab * 8 + (plane - 4) * 4 + block] = 1.0
    return matrix.astype(bf16)


unpack = unpacking()


def product(a, b):
    return lax.dot_general(a, b, (((1,), (0,)), ((), ())), preferred_element_type=f32)


def filter_kernel(occupation, slabs, unpack_rows, high_xy, low_xy, high_z, low_z, out):
    count = 2 * NZ
    left, middle, right = slabs[:, 0:512], slabs[:, 512:1024], slabs[:, 1024:1152]
    first = product(unpack_rows[0:count], left) + product(unpack_rows[6 * NZ : 8 * NZ], middle)
    pieces = product(unpack_rows[count : 6 * NZ], right)
    code = product(unpack_rows[8 * NZ : 9 * NZ], middle) + jnp.concatenate(
        [pieces[block * NZ : block * NZ + NZ] for block in range(4)], axis=1
    )
    levels = jnp.log(code) * (1.0 / (CODE * math.log(2.0))) - OFFSET - 1.5 * stencil_weights[0]
    diagonal = jnp.concatenate([levels, levels], axis=0)
    shifted = diagonal - centre

    def hop(v):
        return (
            product(v, high_xy[...])
            + product(v, low_xy[...])
            + product(high_z[...], v)
            + product(low_z[...], v)
        )

    previous = first
    current = ((hop(first.astype(bf16)) + shifted * first) * (1.0 / spread)).astype(bf16)
    for _ in range(1, DEGREE):
        wide = current.astype(f32)
        following = (hop(current) + shifted * wide) * (2.0 / spread) - previous
        previous = wide
        current = following.astype(bf16)
    applied = (hop(current) + diagonal * current.astype(f32)).astype(bf16)

    row = lax.broadcasted_iota(jnp.int32, (48, count), 0)
    col = lax.broadcasted_iota(jnp.int32, (48, count), 1)
    group = (row >> 1) & 7
    z = THICK * (3 * (group >> 1) + lax.axis_index("zh")) + 3 * (group & 1) + (row >> 4)
    pick = jnp.where(col == (row & 1) * NZ + z, 1.0, 0.0).astype(bf16)
    filtered_rows = product(pick, current).astype(bf16)
    applied_rows = product(pick, applied).astype(bf16)
    for lane_block in range(4):
        lanes = slice(lane_block * 128, lane_block * 128 + 128)
        for p in range(3):
            rows = slice(p * 16, p * 16 + 16)
            target = slice(lane_block * 16, lane_block * 16 + 16)
            out[target, p * 128 : p * 128 + 128] = filtered_rows[rows, lanes]
            out[target, 512 + p * 128 : 640 + p * 128] = applied_rows[rows, lanes]
    state = lax.broadcasted_iota(jnp.int32, (64, 128), 0) & 1
    lane = lax.broadcasted_iota(jnp.int32, (64, 128), 1)
    held = lax.broadcasted_iota(jnp.int32, (1, 8), 1)
    mine = 2 * lax.axis_index("x")
    block = jnp.zeros((64, 128), f32)
    for k in range(2):
        value = jnp.sum(jnp.where(held == mine + k, occupation[...], 0.0), axis=1, keepdims=True)
        for piece in range(3):
            part = value.astype(bf16).astype(f32)
            value = value - part
            block = jnp.where((lane == piece) & (state == k), part, block)
    out[:, 384:512] = block.astype(bf16)


def tile_kernel(own, gathered, out):
    row = lax.broadcasted_iota(jnp.int32, (NS, NS), 0)
    col = lax.broadcasted_iota(jnp.int32, (NS, NS), 1)
    source = ((((row >> 3) & 1) * 4 + ((row >> 1) & 3)) * 32 + (row >> 4)) * 2 + (row & 1)
    order = jnp.where(col == source, 1.0, 0.0).astype(bf16)
    ordered = product(order, gathered[...])
    states = ordered[:, :384]
    occupied = ordered[:, 384:385] + ordered[:, 385:386] + ordered[:, 386:387]
    density = jnp.sum(occupied * (states * states), axis=0, keepdims=True) * (1.0 / NS)

    row = lax.broadcasted_iota(jnp.int32, (128, 128), 0)
    col = lax.broadcasted_iota(jnp.int32, (128, 128), 1)
    source = ((row >> 1) & 1) * 64 + (row >> 2) * 2 + (row & 1)
    interleave = jnp.where(col == source, 1.0, 0.0).astype(bf16)
    stacked = jnp.concatenate([own[:, 512:896], own[:, 0:384]], axis=0)
    left = product(interleave, stacked).astype(bf16)
    tiles = lax.dot_general(
        left, states.astype(bf16), (((1,), (1,)), ((), ())), preferred_element_type=f32
    )
    out[:, 0:512] = tiles.astype(bf16)
    kind = row & 3
    block = jnp.zeros((128, 128), f32)
    for p in range(3):
        block = jnp.where(kind == p, density[:, p * 128 : p * 128 + 128], block)
    high = block.astype(bf16)
    out[:, 512:640] = high
    out[:, 640:768] = (block - high.astype(f32)).astype(bf16)


def sum_kernel(parts, rows, density):
    row = lax.broadcasted_iota(jnp.int32, (4 * SLABS, 128), 0)
    col = lax.broadcasted_iota(jnp.int32, (4 * SLABS, 128), 1)
    adder = jnp.where((row & 3) == (col & 3), 1.0, 0.0).astype(bf16)
    rows[...] = product(adder, parts[:, 0:512]).astype(bf16)
    row = lax.broadcasted_iota(jnp.int32, (8, 128), 0)
    col = lax.broadcasted_iota(jnp.int32, (8, 128), 1)
    half = jnp.where(row >= 3, 1, 0)
    for lane_block in range(4):
        sender = lane_block * 8 + 2 * lax.axis_index("x") + half
        pick = jnp.where((col == sender * 4 + row - 3 * half) & (row < THICK), 1.0, 0.0).astype(bf16)
        lanes = slice(lane_block * 128, lane_block * 128 + 128)
        density[:, lanes] = product(pick, parts[:, 512:640]) + product(pick, parts[:, 640:768])


def final_kernel(received, cells, energy, gram, density):
    rows = received[...].astype(f32)
    scale = 1.0 / (NZ * PLANE)
    for x in range(4):
        total = rows[12 * x : 12 * x + 4] + rows[12 * x + 4 : 12 * x + 8] + rows[12 * x + 8 : 12 * x + 12]
        total = total * scale
        energy[2 * x : 2 * x + 2] = total[0:2]
        gram[2 * x : 2 * x + 2] = total[2:4]
    for line in range(NX):
        density[:, line, :] = cells[0:THICK, line * NY : line * NY + NY]


def exchange(array, axes):
    return lax.all_to_all(array, axes, 0, 0, tiled=True)


def body(orbitals, potential, occupation):
    code = jnp.exp2(CODE * (potential + OFFSET)).astype(bf16)
    wells = jnp.stack([code, code]).reshape(1, 2 * THICK, PLANE)
    rows = jnp.concatenate(
        [orbitals.reshape(4, 2 * THICK, PLANE), jnp.broadcast_to(wells, (4, 2 * THICK, PLANE))], axis=1
    )
    rest = rows[:, 16:18].reshape(4, 8, 128)
    slabs = jnp.concatenate([rows[:, :8], rows[:, 8:16], rest], axis=2)
    slabs = jnp.broadcast_to(slabs[:, None], (4, 3, 8, 1152)).reshape(SLABS, 8, 1152)
    slabs = exchange(slabs, ("x", "zh")).reshape(SLABS * 8, 1152)

    vmem = pl.BlockSpec(memory_space=pltpu.VMEM)
    params = pltpu.CompilerParams(vmem_limit_bytes=24 * 1024 * 1024)
    send = pl.pallas_call(
        filter_kernel,
        out_shape=jax.ShapeDtypeStruct((64, 896), bf16),
        in_specs=[vmem] * 7,
        out_specs=vmem,
        compiler_params=params,
        name="chebyshev",
    )(occupation.reshape(1, 8), slabs, unpack, plane_high, plane_low, depth_high, depth_low)

    own = exchange(send.reshape(32, 2, 896), ("zl", "y")).reshape(64, 896)
    shared = jnp.broadcast_to(own[None, :, :512], (4, 64, 512))
    gathered = exchange(shared, "x").reshape(256, 512)
    gathered = lax.all_gather(gathered, "c", axis=0, tiled=True)

    partial = pl.pallas_call(
        tile_kernel,
        out_shape=jax.ShapeDtypeStruct((128, 768), bf16),
        in_specs=[vmem] * 2,
        out_specs=vmem,
        compiler_params=params,
        name="tiles",
    )(own, gathered)

    parts = exchange(partial.reshape(32, 4, 768), ("zl", "y")).reshape(128, 768)
    rows, cells = pl.pallas_call(
        sum_kernel,
        out_shape=[
            jax.ShapeDtypeStruct((4 * SLABS, NS), bf16),
            jax.ShapeDtypeStruct((8, PLANE), f32),
        ],
        in_specs=[vmem],
        out_specs=[vmem] * 2,
        compiler_params=params,
        name="sums",
    )(parts)

    rows = exchange(rows.reshape(SLABS, 4, NS), ("x", "zh")).reshape(4 * SLABS, NS)
    return pl.pallas_call(
        final_kernel,
        out_shape=[
            jax.ShapeDtypeStruct((8, NS), f32),
            jax.ShapeDtypeStruct((8, NS), f32),
            jax.ShapeDtypeStruct((THICK, NX, NY), f32),
        ],
        in_specs=[vmem] * 2,
        out_specs=[vmem] * 3,
        compiler_params=params,
        name="results",
    )(rows, cells)


def solution(mesh):
    fine = Mesh(mesh.devices.reshape(4, 3, 4, 8, 2), ("x", "zh", "zl", "y", "c"))
    grid, state = ("x", "zh"), ("zl", "y", "c")
    return jax.shard_map(
        body,
        mesh=fine,
        in_specs=(P(state, grid, None, None), P(grid, None, None), P(state)),
        out_specs=(P(state, None), P(state, None), P(grid, None, None)),
        check_vma=False,
    )
```

```python
import math

import jax
import jax.numpy as jnp
import numpy as np
from jax import lax
from jax.experimental import pallas as pl
from jax.experimental.pallas import tpu as pltpu
from jax.sharding import Mesh
from jax.sharding import PartitionSpec as P

NS = 512
RADIUS = 6
DEGREE = 4
NX = 16
NY = 32
NZ = 72
PLANE = NX * NY
SLABS = 12
THICK = NZ // SLABS
PICKED = 9 * NZ + 8

stencil_weights = (
    -5369.0 / 1800.0,
    12.0 / 7.0,
    -15.0 / 56.0,
    10.0 / 189.0,
    -1.0 / 112.0,
    2.0 / 1925.0,
    -1.0 / 16632.0,
)
cut_low = 1.0
cut_high = 12.0
centre = 0.5 * (cut_high + cut_low)
spread = 0.5 * (cut_high - cut_low)
CODE = 120.0
OFFSET = 0.5
bf16 = jnp.bfloat16
f32 = jnp.float32


def ring(count):
    line = np.zeros((count, count))
    rows = np.arange(count)
    for reach in range(1, RADIUS + 1):
        line[rows, (rows + reach) % count] += -0.5 * stencil_weights[reach]
        line[rows, (rows - reach) % count] += -0.5 * stencil_weights[reach]
    return line


def halves(matrix):
    high = matrix.astype(np.float32).astype(bf16)
    low = (matrix - high.astype(np.float64)).astype(np.float32).astype(bf16)
    return high, low


plane_high, plane_low = halves(
    np.kron(ring(NX), np.eye(NY)) + np.kron(np.eye(NX), ring(NY))
)
depth_high, depth_low = halves(np.kron(np.eye(2), ring(NZ)))


def unpacking():
    matrix = np.zeros((PICKED, SLABS * 8), np.float32)
    for slab in range(SLABS):
        for plane in range(THICK):
            z = slab * THICK + plane
            for state in range(2):
                line = state * THICK + plane
                start = 0 if line < 8 else 6 * NZ
                matrix[start + state * NZ + z, slab * 8 + line % 8] = 1.0
            if plane < 4:
                matrix[8 * NZ + z, slab * 8 + 4 + plane] = 1.0
            else:
                for block in range(4):
                    matrix[(2 + block) * NZ + z, slab * 8 + (plane - 4) * 4 + block] = 1.0
    return matrix.astype(bf16)


unpack = unpacking()


def product(a, b):
    return lax.dot_general(a, b, (((1,), (0,)), ((), ())), preferred_element_type=f32)


def filter_kernel(occupation, slabs, unpack_rows, high_xy, low_xy, high_z, low_z, out):
    count = 2 * NZ
    left, middle, right = slabs[:, 0:512], slabs[:, 512:1024], slabs[:, 1024:1152]
    first = product(unpack_rows[0:count], left) + product(unpack_rows[6 * NZ : 8 * NZ], middle)
    pieces = product(unpack_rows[count : 6 * NZ], right)
    code = product(unpack_rows[8 * NZ : PICKED], middle)[:NZ] + jnp.concatenate(
        [pieces[block * NZ : block * NZ + NZ] for block in range(4)], axis=1
    )
    levels = jnp.log(code) * (1.0 / (CODE * math.log(2.0))) - OFFSET - 1.5 * stencil_weights[0]
    diagonal = jnp.concatenate([levels, levels], axis=0)
    shifted = diagonal - centre

    def hop(v):
        return (
            product(v, high_xy[...])
            + product(v, low_xy[...])
            + product(high_z[...], v)
            + product(low_z[...], v)
        )

    previous = first
    current = ((hop(first.astype(bf16)) + shifted * first) * (1.0 / spread)).astype(bf16)
    for _ in range(1, DEGREE):
        wide = current.astype(f32)
        following = (hop(current) + shifted * wide) * (2.0 / spread) - previous
        previous = wide
        current = following.astype(bf16)
    applied = (hop(current) + diagonal * current.astype(f32)).astype(bf16)

    row = lax.broadcasted_iota(jnp.int32, (48, count), 0)
    col = lax.broadcasted_iota(jnp.int32, (48, count), 1)
    group = (row >> 1) & 7
    z = THICK * (3 * (group >> 1) + lax.axis_index("zh")) + 3 * (group & 1) + (row >> 4)
    pick = jnp.where(col == (row & 1) * NZ + z, 1.0, 0.0).astype(bf16)
    filtered_rows = product(pick, current).astype(bf16)
    applied_rows = product(pick, applied).astype(bf16)
    for lane_block in range(4):
        lanes = slice(lane_block * 128, lane_block * 128 + 128)
        for p in range(3):
            rows = slice(p * 16, p * 16 + 16)
            target = slice(lane_block * 16, lane_block * 16 + 16)
            out[target, p * 128 : p * 128 + 128] = filtered_rows[rows, lanes]
            out[target, 512 + p * 128 : 640 + p * 128] = applied_rows[rows, lanes]
    state = lax.broadcasted_iota(jnp.int32, (64, 128), 0) & 1
    lane = lax.broadcasted_iota(jnp.int32, (64, 128), 1)
    held = lax.broadcasted_iota(jnp.int32, (1, 8), 1)
    mine = 2 * lax.axis_index("x")
    block = jnp.zeros((64, 128), f32)
    for k in range(2):
        value = jnp.sum(jnp.where(held == mine + k, occupation[...], 0.0), axis=1, keepdims=True)
        for piece in range(3):
            part = value.astype(bf16).astype(f32)
            value = value - part
            block = jnp.where((lane == piece) & (state == k), part, block)
    out[:, 384:512] = block.astype(bf16)


def tile_kernel(own, gathered, out):
    row = lax.broadcasted_iota(jnp.int32, (NS, NS), 0)
    col = lax.broadcasted_iota(jnp.int32, (NS, NS), 1)
    source = ((((row >> 3) & 1) * 4 + ((row >> 1) & 3)) * 32 + (row >> 4)) * 2 + (row & 1)
    order = jnp.where(col == source, 1.0, 0.0).astype(bf16)
    ordered = product(order, gathered[...])
    states = ordered[:, :384]
    occupied = ordered[:, 384:385] + ordered[:, 385:386] + ordered[:, 386:387]
    density = jnp.sum(occupied * (states * states), axis=0, keepdims=True) * (1.0 / NS)

    row = lax.broadcasted_iota(jnp.int32, (128, 128), 0)
    col = lax.broadcasted_iota(jnp.int32, (128, 128), 1)
    source = ((row >> 1) & 1) * 64 + (row >> 2) * 2 + (row & 1)
    interleave = jnp.where(col == source, 1.0, 0.0).astype(bf16)
    stacked = jnp.concatenate([own[:, 512:896], own[:, 0:384]], axis=0)
    left = product(interleave, stacked).astype(bf16)
    tiles = lax.dot_general(
        left, states.astype(bf16), (((1,), (1,)), ((), ())), preferred_element_type=f32
    )
    out[:, 0:512] = tiles.astype(bf16)
    kind = row & 3
    block = jnp.zeros((128, 128), f32)
    for p in range(3):
        block = jnp.where(kind == p, density[:, p * 128 : p * 128 + 128], block)
    high = block.astype(bf16)
    out[:, 512:640] = high
    out[:, 640:768] = (block - high.astype(f32)).astype(bf16)


def sum_kernel(parts, rows, density):
    row = lax.broadcasted_iota(jnp.int32, (4 * SLABS, 128), 0)
    col = lax.broadcasted_iota(jnp.int32, (4 * SLABS, 128), 1)
    adder = jnp.where((row & 3) == (col & 3), 1.0, 0.0).astype(bf16)
    rows[...] = product(adder, parts[:, 0:512]).astype(bf16)
    row = lax.broadcasted_iota(jnp.int32, (8, 128), 0)
    col = lax.broadcasted_iota(jnp.int32, (8, 128), 1)
    half = jnp.where(row >= 3, 1, 0)
    for lane_block in range(4):
        sender = lane_block * 8 + 2 * lax.axis_index("x") + half
        pick = jnp.where((col == sender * 4 + row - 3 * half) & (row < THICK), 1.0, 0.0).astype(bf16)
        lanes = slice(lane_block * 128, lane_block * 128 + 128)
        density[:, lanes] = product(pick, parts[:, 512:640]) + product(pick, parts[:, 640:768])


def final_kernel(received, cells, energy, gram, density):
    rows = received[...].astype(f32)
    scale = 1.0 / (NZ * PLANE)
    for x in range(4):
        total = rows[12 * x : 12 * x + 4] + rows[12 * x + 4 : 12 * x + 8] + rows[12 * x + 8 : 12 * x + 12]
        total = total * scale
        energy[2 * x : 2 * x + 2] = total[0:2]
        gram[2 * x : 2 * x + 2] = total[2:4]
    for line in range(NX):
        density[:, line, :] = cells[0:THICK, line * NY : line * NY + NY]


def exchange(array, axes):
    return lax.all_to_all(array, axes, 0, 0, tiled=True)


def body(orbitals, potential, occupation):
    code = jnp.exp2(CODE * (potential + OFFSET)).astype(bf16)
    wells = jnp.stack([code, code]).reshape(1, 2 * THICK, PLANE)
    rows = jnp.concatenate(
        [orbitals.reshape(4, 2 * THICK, PLANE), jnp.broadcast_to(wells, (4, 2 * THICK, PLANE))], axis=1
    )
    rest = rows[:, 16:18].reshape(4, 8, 128)
    slabs = jnp.concatenate([rows[:, :8], rows[:, 8:16], rest], axis=2)
    slabs = jnp.broadcast_to(slabs[:, None], (4, 3, 8, 1152)).reshape(SLABS, 8, 1152)
    slabs = exchange(slabs, ("x", "zh")).reshape(SLABS * 8, 1152)

    vmem = pl.BlockSpec(memory_space=pltpu.VMEM)
    params = pltpu.CompilerParams(vmem_limit_bytes=24 * 1024 * 1024)
    send = pl.pallas_call(
        filter_kernel,
        out_shape=jax.ShapeDtypeStruct((64, 896), bf16),
        in_specs=[vmem] * 7,
        out_specs=vmem,
        compiler_params=params,
        name="chebyshev",
    )(occupation.reshape(1, 8), slabs, unpack, plane_high, plane_low, depth_high, depth_low)

    own = exchange(send.reshape(32, 2, 896), ("zl", "y")).reshape(64, 896)
    shared = jnp.broadcast_to(own[None, :, :512], (4, 64, 512))
    gathered = exchange(shared, "x").reshape(256, 512)
    gathered = lax.all_gather(gathered, "c", axis=0, tiled=True)

    partial = pl.pallas_call(
        tile_kernel,
        out_shape=jax.ShapeDtypeStruct((128, 768), bf16),
        in_specs=[vmem] * 2,
        out_specs=vmem,
        compiler_params=params,
        name="tiles",
    )(own, gathered)

    parts = exchange(partial.reshape(32, 4, 768), ("zl", "y")).reshape(128, 768)
    rows, cells = pl.pallas_call(
        sum_kernel,
        out_shape=[
            jax.ShapeDtypeStruct((4 * SLABS, NS), bf16),
            jax.ShapeDtypeStruct((8, PLANE), f32),
        ],
        in_specs=[vmem],
        out_specs=[vmem] * 2,
        compiler_params=params,
        name="sums",
    )(parts)

    rows = exchange(rows.reshape(SLABS, 4, NS), ("x", "zh")).reshape(4 * SLABS, NS)
    return pl.pallas_call(
        final_kernel,
        out_shape=[
            jax.ShapeDtypeStruct((8, NS), f32),
            jax.ShapeDtypeStruct((8, NS), f32),
            jax.ShapeDtypeStruct((THICK, NX, NY), f32),
        ],
        in_specs=[vmem] * 2,
        out_specs=[vmem] * 3,
        compiler_params=params,
        name="results",
    )(rows, cells)


def solution(mesh):
    fine = Mesh(mesh.devices.reshape(4, 3, 4, 8, 2), ("x", "zh", "zl", "y", "c"))
    grid, state = ("x", "zh"), ("zl", "y", "c")
    return jax.shard_map(
        body,
        mesh=fine,
        in_specs=(P(state, grid, None, None), P(grid, None, None), P(state)),
        out_specs=(P(state, None), P(state, None), P(grid, None, None)),
        check_vma=False,
    )
```

```python
import math

import jax
import jax.numpy as jnp
import numpy as np
from jax import lax
from jax.experimental import pallas as pl
from jax.experimental.pallas import tpu as pltpu
from jax.sharding import Mesh
from jax.sharding import PartitionSpec as P

NS = 512
RADIUS = 6
DEGREE = 4
NX = 16
NY = 32
NZ = 72
PLANE = NX * NY
SLABS = 12
THICK = NZ // SLABS
PICKED = 9 * NZ + 8

stencil_weights = (
    -5369.0 / 1800.0,
    12.0 / 7.0,
    -15.0 / 56.0,
    10.0 / 189.0,
    -1.0 / 112.0,
    2.0 / 1925.0,
    -1.0 / 16632.0,
)
cut_low = 1.0
cut_high = 12.0
centre = 0.5 * (cut_high + cut_low)
spread = 0.5 * (cut_high - cut_low)
CODE = 120.0
OFFSET = 0.5
bf16 = jnp.bfloat16
f32 = jnp.float32


def ring(count):
    line = np.zeros((count, count))
    rows = np.arange(count)
    for reach in range(1, RADIUS + 1):
        line[rows, (rows + reach) % count] += -0.5 * stencil_weights[reach]
        line[rows, (rows - reach) % count] += -0.5 * stencil_weights[reach]
    return line


def halves(matrix):
    high = matrix.astype(np.float32).astype(bf16)
    low = (matrix - high.astype(np.float64)).astype(np.float32).astype(bf16)
    return high, low


plane_high, plane_low = halves(
    np.kron(ring(NX), np.eye(NY)) + np.kron(np.eye(NX), ring(NY))
)
depth_high, depth_low = halves(np.kron(np.eye(2), ring(NZ)))


def unpacking():
    matrix = np.zeros((PICKED, SLABS * 8), np.float32)
    for slab in range(SLABS):
        for plane in range(THICK):
            z = slab * THICK + plane
            for state in range(2):
                line = state * THICK + plane
                start = 0 if line < 8 else 6 * NZ
                matrix[start + state * NZ + z, slab * 8 + line % 8] = 1.0
            if plane < 4:
                matrix[8 * NZ + z, slab * 8 + 4 + plane] = 1.0
            else:
                for block in range(4):
                    matrix[(2 + block) * NZ + z, slab * 8 + (plane - 4) * 4 + block] = 1.0
    return matrix.astype(bf16)


unpack = unpacking()


def slab_of(line):
    return sum(jnp.where(line >= THICK * slab, 1, 0) for slab in range(1, 4))


def product(a, b):
    return lax.dot_general(a, b, (((1,), (0,)), ((), ())), preferred_element_type=f32)


def filter_kernel(occupation, slabs, unpack_rows, high_xy, low_xy, high_z, low_z, out):
    count = 2 * NZ
    left, middle, right = slabs[:, 0:512], slabs[:, 512:1024], slabs[:, 1024:1152]
    first = product(unpack_rows[0:count], left) + product(unpack_rows[6 * NZ : 8 * NZ], middle)
    pieces = product(unpack_rows[count : 6 * NZ], right)
    code = product(unpack_rows[8 * NZ : PICKED], middle)[:NZ] + jnp.concatenate(
        [pieces[block * NZ : block * NZ + NZ] for block in range(4)], axis=1
    )
    levels = jnp.log(code) * (1.0 / (CODE * math.log(2.0))) - OFFSET - 1.5 * stencil_weights[0]
    diagonal = jnp.concatenate([levels, levels], axis=0)
    shifted = diagonal - centre

    def hop(v):
        return (
            product(v, high_xy[...])
            + product(v, low_xy[...])
            + product(high_z[...], v)
            + product(low_z[...], v)
        )

    previous = first
    current = ((hop(first.astype(bf16)) + shifted * first) * (1.0 / spread)).astype(bf16)
    for _ in range(1, DEGREE):
        wide = current.astype(f32)
        following = (hop(current) + shifted * wide) * (2.0 / spread) - previous
        previous = wide
        current = following.astype(bf16)
    applied = (hop(current) + diagonal * current.astype(f32)).astype(bf16)

    row = lax.broadcasted_iota(jnp.int32, (48, count), 0)
    col = lax.broadcasted_iota(jnp.int32, (48, count), 1)
    line = ((row >> 1) & 7) + 8 * (row >> 4)
    slab = slab_of(line)
    z = THICK * (3 * slab + lax.axis_index("zh")) + line - THICK * slab
    pick = jnp.where(col == (row & 1) * NZ + z, 1.0, 0.0).astype(bf16)
    filtered_rows = product(pick, current).astype(bf16)
    applied_rows = product(pick, applied).astype(bf16)
    for lane_block in range(4):
        lanes = slice(lane_block * 128, lane_block * 128 + 128)
        for p in range(3):
            rows = slice(p * 16, p * 16 + 16)
            target = slice(lane_block * 16, lane_block * 16 + 16)
            out[target, p * 128 : p * 128 + 128] = filtered_rows[rows, lanes]
            out[target, 512 + p * 128 : 640 + p * 128] = applied_rows[rows, lanes]
    state = lax.broadcasted_iota(jnp.int32, (64, 128), 0) & 1
    lane = lax.broadcasted_iota(jnp.int32, (64, 128), 1)
    held = lax.broadcasted_iota(jnp.int32, (1, 8), 1)
    mine = 2 * lax.axis_index("x")
    block = jnp.zeros((64, 128), f32)
    for k in range(2):
        value = jnp.sum(jnp.where(held == mine + k, occupation[...], 0.0), axis=1, keepdims=True)
        for piece in range(3):
            part = value.astype(bf16).astype(f32)
            value = value - part
            block = jnp.where((lane == piece) & (state == k), part, block)
    out[:, 384:512] = block.astype(bf16)


def tile_kernel(own, gathered, out):
    row = lax.broadcasted_iota(jnp.int32, (NS, NS), 0)
    col = lax.broadcasted_iota(jnp.int32, (NS, NS), 1)
    source = ((((row >> 3) & 1) * 4 + ((row >> 1) & 3)) * 32 + (row >> 4)) * 2 + (row & 1)
    order = jnp.where(col == source, 1.0, 0.0).astype(bf16)
    ordered = product(order, gathered[...])
    states = ordered[:, :384]
    occupied = ordered[:, 384:385] + ordered[:, 385:386] + ordered[:, 386:387]
    density = jnp.sum(occupied * (states * states), axis=0, keepdims=True) * (1.0 / NS)

    row = lax.broadcasted_iota(jnp.int32, (128, 128), 0)
    col = lax.broadcasted_iota(jnp.int32, (128, 128), 1)
    source = ((row >> 1) & 1) * 64 + (row >> 2) * 2 + (row & 1)
    interleave = jnp.where(col == source, 1.0, 0.0).astype(bf16)
    stacked = jnp.concatenate([own[:, 512:896], own[:, 0:384]], axis=0)
    left = product(interleave, stacked).astype(bf16)
    tiles = lax.dot_general(
        left, states.astype(bf16), (((1,), (1,)), ((), ())), preferred_element_type=f32
    )
    out[:, 0:512] = tiles.astype(bf16)
    cells = jnp.zeros((1, 128), f32)
    for p in range(3):
        mine = slab_of(lax.axis_index("y") + 8 * p) == lax.axis_index("x")
        cells = jnp.where(mine, density[:, p * 128 : p * 128 + 128], cells)
    high = cells.astype(bf16).astype(f32)
    kind = row & 3
    block = jnp.where(kind == 0, high, jnp.where(kind == 1, cells - high, 0.0))
    out[:, 512:640] = block.astype(bf16)


def sum_kernel(parts, rows, density):
    row = lax.broadcasted_iota(jnp.int32, (4 * SLABS, 128), 0)
    col = lax.broadcasted_iota(jnp.int32, (4 * SLABS, 128), 1)
    adder = jnp.where((row & 3) == (col & 3), 1.0, 0.0).astype(bf16)
    rows[...] = product(adder, parts[:, 0:512]).astype(bf16)
    row = lax.broadcasted_iota(jnp.int32, (8, 128), 0)
    col = lax.broadcasted_iota(jnp.int32, (8, 128), 1)
    for lane_block in range(4):
        sender = lane_block * 8 + ((THICK * lax.axis_index("x") + row) & 7)
        hit = ((col == sender * 4) | (col == sender * 4 + 1)) & (row < THICK)
        pick = jnp.where(hit, 1.0, 0.0).astype(bf16)
        lanes = slice(lane_block * 128, lane_block * 128 + 128)
        density[:, lanes] = product(pick, parts[:, 512:640])


def final_kernel(received, cells, energy, gram, density):
    rows = received[...].astype(f32)
    scale = 1.0 / (NZ * PLANE)
    for x in range(4):
        total = rows[12 * x : 12 * x + 4] + rows[12 * x + 4 : 12 * x + 8] + rows[12 * x + 8 : 12 * x + 12]
        total = total * scale
        energy[2 * x : 2 * x + 2] = total[0:2]
        gram[2 * x : 2 * x + 2] = total[2:4]
    for line in range(NX):
        density[:, line, :] = cells[0:THICK, line * NY : line * NY + NY]


def exchange(array, axes):
    return lax.all_to_all(array, axes, 0, 0, tiled=True)


def body(orbitals, potential, occupation):
    code = jnp.exp2(CODE * (potential + OFFSET)).astype(bf16)
    wells = jnp.stack([code, code]).reshape(1, 2 * THICK, PLANE)
    rows = jnp.concatenate(
        [orbitals.reshape(4, 2 * THICK, PLANE), jnp.broadcast_to(wells, (4, 2 * THICK, PLANE))], axis=1
    )
    rest = rows[:, 16:18].reshape(4, 8, 128)
    slabs = jnp.concatenate([rows[:, :8], rows[:, 8:16], rest], axis=2)
    slabs = jnp.broadcast_to(slabs[:, None], (4, 3, 8, 1152)).reshape(SLABS, 8, 1152)
    slabs = exchange(slabs, ("x", "zh")).reshape(SLABS * 8, 1152)

    vmem = pl.BlockSpec(memory_space=pltpu.VMEM)
    params = pltpu.CompilerParams(vmem_limit_bytes=24 * 1024 * 1024)
    send = pl.pallas_call(
        filter_kernel,
        out_shape=jax.ShapeDtypeStruct((64, 896), bf16),
        in_specs=[vmem] * 7,
        out_specs=vmem,
        compiler_params=params,
        name="chebyshev",
    )(occupation.reshape(1, 8), slabs, unpack, plane_high, plane_low, depth_high, depth_low)

    own = exchange(send.reshape(32, 2, 896), ("zl", "y")).reshape(64, 896)
    shared = jnp.broadcast_to(own[None, :, :512], (4, 64, 512))
    gathered = exchange(shared, "x").reshape(256, 512)
    gathered = lax.all_gather(gathered, "c", axis=0, tiled=True)

    partial = pl.pallas_call(
        tile_kernel,
        out_shape=jax.ShapeDtypeStruct((128, 640), bf16),
        in_specs=[vmem] * 2,
        out_specs=vmem,
        compiler_params=params,
        name="tiles",
    )(own, gathered)

    parts = exchange(partial.reshape(32, 4, 640), ("zl", "y")).reshape(128, 640)
    rows, cells = pl.pallas_call(
        sum_kernel,
        out_shape=[
            jax.ShapeDtypeStruct((4 * SLABS, NS), bf16),
            jax.ShapeDtypeStruct((8, PLANE), f32),
        ],
        in_specs=[vmem],
        out_specs=[vmem] * 2,
        compiler_params=params,
        name="sums",
    )(parts)

    rows = exchange(rows.reshape(SLABS, 4, NS), ("x", "zh")).reshape(4 * SLABS, NS)
    return pl.pallas_call(
        final_kernel,
        out_shape=[
            jax.ShapeDtypeStruct((8, NS), f32),
            jax.ShapeDtypeStruct((8, NS), f32),
            jax.ShapeDtypeStruct((THICK, NX, NY), f32),
        ],
        in_specs=[vmem] * 2,
        out_specs=[vmem] * 3,
        compiler_params=params,
        name="results",
    )(rows, cells)


def solution(mesh):
    fine = Mesh(mesh.devices.reshape(4, 3, 4, 8, 2), ("x", "zh", "zl", "y", "c"))
    grid, state = ("x", "zh"), ("zl", "y", "c")
    return jax.shard_map(
        body,
        mesh=fine,
        in_specs=(P(state, grid, None, None), P(grid, None, None), P(state)),
        out_specs=(P(state, None), P(state, None), P(grid, None, None)),
        check_vma=False,
    )
```

```python
import math

import jax
import jax.numpy as jnp
import numpy as np
from jax import lax
from jax.experimental import pallas as pl
from jax.experimental.pallas import tpu as pltpu
from jax.sharding import Mesh
from jax.sharding import PartitionSpec as P

NS = 512
RADIUS = 6
DEGREE = 4
NX = 16
NY = 32
NZ = 72
PLANE = NX * NY
SLABS = 12
THICK = NZ // SLABS
PICKED = 9 * NZ + 8

stencil_weights = (
    -5369.0 / 1800.0,
    12.0 / 7.0,
    -15.0 / 56.0,
    10.0 / 189.0,
    -1.0 / 112.0,
    2.0 / 1925.0,
    -1.0 / 16632.0,
)
cut_low = 1.0
cut_high = 12.0
centre = 0.5 * (cut_high + cut_low)
spread = 0.5 * (cut_high - cut_low)
CODE = 120.0
OFFSET = 0.5
bf16 = jnp.bfloat16
f32 = jnp.float32


def ring(count):
    line = np.zeros((count, count))
    rows = np.arange(count)
    for reach in range(1, RADIUS + 1):
        line[rows, (rows + reach) % count] += -0.5 * stencil_weights[reach]
        line[rows, (rows - reach) % count] += -0.5 * stencil_weights[reach]
    return line


def halves(matrix):
    high = matrix.astype(np.float32).astype(bf16)
    low = (matrix - high.astype(np.float64)).astype(np.float32).astype(bf16)
    return high, low


plane_high, plane_low = halves(
    np.kron(ring(NX), np.eye(NY)) + np.kron(np.eye(NX), ring(NY))
)
depth_high, depth_low = halves(np.kron(np.eye(2), ring(NZ)))


def unpacking():
    matrix = np.zeros((PICKED, SLABS * 8), np.float32)
    for slab in range(SLABS):
        for plane in range(THICK):
            z = slab * THICK + plane
            for state in range(2):
                line = state * THICK + plane
                start = 0 if line < 8 else 6 * NZ
                matrix[start + state * NZ + z, slab * 8 + line % 8] = 1.0
            if plane < 4:
                matrix[8 * NZ + z, slab * 8 + 4 + plane] = 1.0
            else:
                for block in range(4):
                    matrix[(2 + block) * NZ + z, slab * 8 + (plane - 4) * 4 + block] = 1.0
    return matrix.astype(bf16)


unpack = unpacking()


def slab_of(line):
    return sum(jnp.where(line >= THICK * slab, 1, 0) for slab in range(1, 4))


def product(a, b):
    return lax.dot_general(a, b, (((1,), (0,)), ((), ())), preferred_element_type=f32)


def filter_kernel(occupation, slabs, unpack_rows, high_xy, low_xy, high_z, low_z, out):
    count = 2 * NZ
    left, middle, right = slabs[:, 0:512], slabs[:, 512:1024], slabs[:, 1024:1152]
    first = product(unpack_rows[0:count], left) + product(unpack_rows[6 * NZ : 8 * NZ], middle)
    pieces = product(unpack_rows[count : 6 * NZ], right)
    code = product(unpack_rows[8 * NZ : PICKED], middle)[:NZ] + jnp.concatenate(
        [pieces[block * NZ : block * NZ + NZ] for block in range(4)], axis=1
    )
    levels = jnp.log(code) * (1.0 / (CODE * math.log(2.0))) - OFFSET - 1.5 * stencil_weights[0]
    diagonal = jnp.concatenate([levels, levels], axis=0)
    shifted = diagonal - centre

    def hop(v):
        return (
            product(v, high_xy[...])
            + product(v, low_xy[...])
            + product(high_z[...], v)
            + product(low_z[...], v)
        )

    previous = first
    current = ((hop(first.astype(bf16)) + shifted * first) * (1.0 / spread)).astype(bf16)
    for _ in range(1, DEGREE):
        wide = current.astype(f32)
        following = (hop(current) + shifted * wide) * (2.0 / spread) - previous
        previous = wide
        current = following.astype(bf16)
    applied = (hop(current) + diagonal * current.astype(f32)).astype(bf16)

    row = lax.broadcasted_iota(jnp.int32, (48, count), 0)
    col = lax.broadcasted_iota(jnp.int32, (48, count), 1)
    line = ((row >> 1) & 7) + 8 * (row >> 4)
    slab = slab_of(line)
    z = THICK * (3 * slab + lax.axis_index("zh")) + line - THICK * slab
    pick = jnp.where(col == (row & 1) * NZ + z, 1.0, 0.0).astype(bf16)
    filtered_rows = product(pick, current).astype(bf16)
    applied_rows = product(pick, applied).astype(bf16)
    for lane_block in range(4):
        lanes = slice(lane_block * 128, lane_block * 128 + 128)
        for p in range(3):
            rows = slice(p * 16, p * 16 + 16)
            target = slice(lane_block * 16, lane_block * 16 + 16)
            out[target, p * 128 : p * 128 + 128] = filtered_rows[rows, lanes]
            out[target, 512 + p * 128 : 640 + p * 128] = applied_rows[rows, lanes]
    lane = lax.broadcasted_iota(jnp.int32, (8, 128), 1)
    held = lax.broadcasted_iota(jnp.int32, (8, 128), 0)
    value = jnp.sum(
        jnp.where(held[:, 0:8] == lane[:, 0:8], occupation[...], 0.0), axis=1, keepdims=True
    )
    block = jnp.zeros((8, 128), f32)
    for piece in range(3):
        part = value.astype(bf16).astype(f32)
        value = value - part
        block = jnp.where(lane == 8 * piece + held, part, block)
    block = jnp.sum(block, axis=0, keepdims=True)
    out[:, 384:512] = jnp.broadcast_to(block, (64, 128)).astype(bf16)


def tile_kernel(own, gathered, out):
    row = lax.broadcasted_iota(jnp.int32, (NS, NS), 0)
    col = lax.broadcasted_iota(jnp.int32, (NS, NS), 1)
    source = ((row >> 3) & 1) * 256 + ((row >> 1) & 3) * 64 + (row >> 4) * 2 + (row & 1)
    order = jnp.where(col == source, 1.0, 0.0).astype(bf16)
    states = product(order, jnp.concatenate([gathered[0:256], gathered[320:576]], axis=0))
    held = lax.broadcasted_iota(jnp.int32, (NS, 128), 0)
    lane = lax.broadcasted_iota(jnp.int32, (NS, 128), 1)
    owner = jnp.where(lane == ((held >> 3) & 1) * 64 + (held >> 4) * 2, 1.0, 0.0).astype(bf16)
    pieces = product(
        owner, jnp.concatenate([gathered[256:320, 0:128], gathered[576:640, 0:128]], axis=0)
    )
    wanted = ((lane & 7) == (held & 7)) & (lane < 24)
    occupied = jnp.sum(jnp.where(wanted, pieces, 0.0), axis=1, keepdims=True)
    density = jnp.sum(occupied * (states * states), axis=0, keepdims=True) * (1.0 / NS)

    row = lax.broadcasted_iota(jnp.int32, (128, 128), 0)
    col = lax.broadcasted_iota(jnp.int32, (128, 128), 1)
    source = ((row >> 1) & 1) * 64 + (row >> 2) * 2 + (row & 1)
    interleave = jnp.where(col == source, 1.0, 0.0).astype(bf16)
    stacked = jnp.concatenate([own[:, 512:896], own[:, 0:384]], axis=0)
    left = product(interleave, stacked).astype(bf16)
    tiles = lax.dot_general(
        left, states.astype(bf16), (((1,), (1,)), ((), ())), preferred_element_type=f32
    )
    out[:, 0:512] = tiles.astype(bf16)
    cells = jnp.zeros((1, 128), f32)
    for p in range(3):
        mine = slab_of(lax.axis_index("y") + 8 * p) == lax.axis_index("x")
        cells = jnp.where(mine, density[:, p * 128 : p * 128 + 128], cells)
    high = cells.astype(bf16).astype(f32)
    kind = row & 3
    block = jnp.where(kind == 0, high, jnp.where(kind == 1, cells - high, 0.0))
    out[:, 512:640] = block.astype(bf16)


def sum_kernel(parts, rows, density):
    row = lax.broadcasted_iota(jnp.int32, (4 * SLABS, 128), 0)
    col = lax.broadcasted_iota(jnp.int32, (4 * SLABS, 128), 1)
    adder = jnp.where((row & 3) == (col & 3), 1.0, 0.0).astype(bf16)
    rows[...] = product(adder, parts[:, 0:512]).astype(bf16)
    row = lax.broadcasted_iota(jnp.int32, (8, 128), 0)
    col = lax.broadcasted_iota(jnp.int32, (8, 128), 1)
    for lane_block in range(4):
        sender = lane_block * 8 + ((THICK * lax.axis_index("x") + row) & 7)
        hit = ((col == sender * 4) | (col == sender * 4 + 1)) & (row < THICK)
        pick = jnp.where(hit, 1.0, 0.0).astype(bf16)
        lanes = slice(lane_block * 128, lane_block * 128 + 128)
        density[:, lanes] = product(pick, parts[:, 512:640])


def final_kernel(received, cells, energy, gram, density):
    rows = received[...].astype(f32)
    scale = 1.0 / (NZ * PLANE)
    for x in range(4):
        total = rows[12 * x : 12 * x + 4] + rows[12 * x + 4 : 12 * x + 8] + rows[12 * x + 8 : 12 * x + 12]
        total = total * scale
        energy[2 * x : 2 * x + 2] = total[0:2]
        gram[2 * x : 2 * x + 2] = total[2:4]
    for line in range(NX):
        density[:, line, :] = cells[0:THICK, line * NY : line * NY + NY]


def exchange(array, axes):
    return lax.all_to_all(array, axes, 0, 0, tiled=True)


def body(orbitals, potential, occupation):
    code = jnp.exp2(CODE * (potential + OFFSET)).astype(bf16)
    wells = jnp.stack([code, code]).reshape(1, 2 * THICK, PLANE)
    rows = jnp.concatenate(
        [orbitals.reshape(4, 2 * THICK, PLANE), jnp.broadcast_to(wells, (4, 2 * THICK, PLANE))], axis=1
    )
    rest = rows[:, 16:18].reshape(4, 8, 128)
    slabs = jnp.concatenate([rows[:, :8], rows[:, 8:16], rest], axis=2)
    slabs = jnp.broadcast_to(slabs[:, None], (4, 3, 8, 1152)).reshape(SLABS, 8, 1152)
    slabs = exchange(slabs, ("x", "zh")).reshape(SLABS * 8, 1152)

    vmem = pl.BlockSpec(memory_space=pltpu.VMEM)
    params = pltpu.CompilerParams(vmem_limit_bytes=24 * 1024 * 1024)
    send = pl.pallas_call(
        filter_kernel,
        out_shape=jax.ShapeDtypeStruct((64, 896), bf16),
        in_specs=[vmem] * 7,
        out_specs=vmem,
        compiler_params=params,
        name="chebyshev",
    )(occupation.reshape(1, 8), slabs, unpack, plane_high, plane_low, depth_high, depth_low)

    own = exchange(send.reshape(32, 2, 896), ("zl", "y")).reshape(64, 896)
    shared = jnp.broadcast_to(own[None, :, :384], (4, 64, 384))
    gathered = exchange(shared, "x").reshape(256, 384)
    gathered, late = lax.optimization_barrier((gathered, own))
    occupied = jnp.pad(late[:, 384:512], ((0, 0), (0, 256)))
    gathered = jnp.concatenate([gathered, occupied], axis=0)
    gathered = lax.all_gather(gathered, "c", axis=0, tiled=True)

    partial = pl.pallas_call(
        tile_kernel,
        out_shape=jax.ShapeDtypeStruct((128, 640), bf16),
        in_specs=[vmem] * 2,
        out_specs=vmem,
        compiler_params=params,
        name="tiles",
    )(own, gathered)

    parts = exchange(partial.reshape(32, 4, 640), ("zl", "y")).reshape(128, 640)
    rows, cells = pl.pallas_call(
        sum_kernel,
        out_shape=[
            jax.ShapeDtypeStruct((4 * SLABS, NS), bf16),
            jax.ShapeDtypeStruct((8, PLANE), f32),
        ],
        in_specs=[vmem],
        out_specs=[vmem] * 2,
        compiler_params=params,
        name="sums",
    )(parts)

    rows = exchange(rows.reshape(SLABS, 4, NS), ("x", "zh")).reshape(4 * SLABS, NS)
    return pl.pallas_call(
        final_kernel,
        out_shape=[
            jax.ShapeDtypeStruct((8, NS), f32),
            jax.ShapeDtypeStruct((8, NS), f32),
            jax.ShapeDtypeStruct((THICK, NX, NY), f32),
        ],
        in_specs=[vmem] * 2,
        out_specs=[vmem] * 3,
        compiler_params=params,
        name="results",
    )(rows, cells)


def solution(mesh):
    fine = Mesh(mesh.devices.reshape(4, 3, 4, 8, 2), ("x", "zh", "zl", "y", "c"))
    grid, state = ("x", "zh"), ("zl", "y", "c")
    return jax.shard_map(
        body,
        mesh=fine,
        in_specs=(P(state, grid, None, None), P(grid, None, None), P(state)),
        out_specs=(P(state, None), P(state, None), P(grid, None, None)),
        check_vma=False,
    )
```

```python
import math

import jax
import jax.numpy as jnp
import numpy as np
from jax import lax
from jax.experimental import pallas as pl
from jax.experimental.pallas import tpu as pltpu
from jax.sharding import Mesh
from jax.sharding import PartitionSpec as P

NS = 512
RADIUS = 6
DEGREE = 4
NX = 16
NY = 32
NZ = 72
PLANE = NX * NY
SLABS = 12
THICK = NZ // SLABS
PICKED = 9 * NZ + 8

stencil_weights = (
    -5369.0 / 1800.0,
    12.0 / 7.0,
    -15.0 / 56.0,
    10.0 / 189.0,
    -1.0 / 112.0,
    2.0 / 1925.0,
    -1.0 / 16632.0,
)
cut_low = 1.0
cut_high = 12.0
centre = 0.5 * (cut_high + cut_low)
spread = 0.5 * (cut_high - cut_low)
CODE = 120.0
OFFSET = 0.5
bf16 = jnp.bfloat16
f32 = jnp.float32


def ring(count):
    line = np.zeros((count, count))
    rows = np.arange(count)
    for reach in range(1, RADIUS + 1):
        line[rows, (rows + reach) % count] += -0.5 * stencil_weights[reach]
        line[rows, (rows - reach) % count] += -0.5 * stencil_weights[reach]
    return line


def halves(matrix):
    high = matrix.astype(np.float32).astype(bf16)
    low = (matrix - high.astype(np.float64)).astype(np.float32).astype(bf16)
    return high, low


plane_high, plane_low = halves(
    np.kron(ring(NX), np.eye(NY)) + np.kron(np.eye(NX), ring(NY))
)
depth_high, depth_low = halves(np.kron(np.eye(2), ring(NZ)))


def unpacking():
    matrix = np.zeros((PICKED, SLABS * 8), np.float32)
    for slab in range(SLABS):
        for plane in range(THICK):
            z = slab * THICK + plane
            for state in range(2):
                line = state * THICK + plane
                start = 0 if line < 8 else 6 * NZ
                matrix[start + state * NZ + z, slab * 8 + line % 8] = 1.0
            if plane < 4:
                matrix[8 * NZ + z, slab * 8 + 4 + plane] = 1.0
            else:
                for block in range(4):
                    matrix[(2 + block) * NZ + z, slab * 8 + (plane - 4) * 4 + block] = 1.0
    return matrix.astype(bf16)


unpack = unpacking()


def slab_of(line):
    return sum(jnp.where(line >= THICK * slab, 1, 0) for slab in range(1, 4))


def product(a, b):
    return lax.dot_general(a, b, (((1,), (0,)), ((), ())), preferred_element_type=f32)


def filter_kernel(occupation, slabs, unpack_rows, high_xy, low_xy, high_z, low_z, out):
    count = 2 * NZ
    left, middle, right = slabs[:, 0:512], slabs[:, 512:1024], slabs[:, 1024:1152]
    first = product(unpack_rows[0:count], left) + product(unpack_rows[6 * NZ : 8 * NZ], middle)
    pieces = product(unpack_rows[count : 6 * NZ], right)
    code = product(unpack_rows[8 * NZ : PICKED], middle)[:NZ] + jnp.concatenate(
        [pieces[block * NZ : block * NZ + NZ] for block in range(4)], axis=1
    )
    levels = jnp.log(code) * (1.0 / (CODE * math.log(2.0))) - OFFSET - 1.5 * stencil_weights[0]
    diagonal = jnp.concatenate([levels, levels], axis=0)
    shifted = diagonal - centre

    def hop(v):
        return (
            product(v, high_xy[...])
            + product(v, low_xy[...])
            + product(high_z[...], v)
            + product(low_z[...], v)
        )

    previous = first
    current = ((hop(first.astype(bf16)) + shifted * first) * (1.0 / spread)).astype(bf16)
    for _ in range(1, DEGREE):
        wide = current.astype(f32)
        following = (hop(current) + shifted * wide) * (2.0 / spread) - previous
        previous = wide
        current = following.astype(bf16)
    applied = (hop(current) + diagonal * current.astype(f32)).astype(bf16)

    row = lax.broadcasted_iota(jnp.int32, (48, count), 0)
    col = lax.broadcasted_iota(jnp.int32, (48, count), 1)
    line = ((row >> 1) & 7) + 8 * (row >> 4)
    slab = slab_of(line)
    z = THICK * (3 * slab + lax.axis_index("zh")) + line - THICK * slab
    pick = jnp.where(col == (row & 1) * NZ + z, 1.0, 0.0).astype(bf16)
    filtered_rows = product(pick, current).astype(bf16)
    applied_rows = product(pick, applied).astype(bf16)
    for lane_block in range(4):
        lanes = slice(lane_block * 128, lane_block * 128 + 128)
        for p in range(3):
            rows = slice(p * 16, p * 16 + 16)
            target = slice(lane_block * 16, lane_block * 16 + 16)
            out[target, p * 128 : p * 128 + 128] = filtered_rows[rows, lanes]
            out[target, 512 + p * 128 : 640 + p * 128] = applied_rows[rows, lanes]
    lane = lax.broadcasted_iota(jnp.int32, (8, 128), 1)
    held = lax.broadcasted_iota(jnp.int32, (8, 128), 0)
    value = jnp.sum(
        jnp.where(held[:, 0:8] == lane[:, 0:8], occupation[...], 0.0), axis=1, keepdims=True
    )
    block = jnp.zeros((8, 128), f32)
    for piece in range(3):
        part = value.astype(bf16).astype(f32)
        value = value - part
        block = jnp.where(lane == 8 * piece + held, part, block)
    block = jnp.sum(block, axis=0, keepdims=True)
    out[:, 384:512] = jnp.broadcast_to(block, (64, 128)).astype(bf16)


def tile_kernel(own, gathered, out):
    row = lax.broadcasted_iota(jnp.int32, (NS, NS), 0)
    col = lax.broadcasted_iota(jnp.int32, (NS, NS), 1)
    source = ((row >> 3) & 1) * 256 + ((row >> 1) & 3) * 64 + (row >> 4) * 2 + (row & 1)
    order = jnp.where(col == source, 1.0, 0.0).astype(bf16)
    states = product(order, jnp.concatenate([gathered[0:256], gathered[320:576]], axis=0))
    held = lax.broadcasted_iota(jnp.int32, (NS, 128), 0)
    lane = lax.broadcasted_iota(jnp.int32, (NS, 128), 1)
    owner = jnp.where(lane == ((held >> 3) & 1) * 64 + (held >> 4) * 2, 1.0, 0.0).astype(bf16)
    pieces = product(
        owner, jnp.concatenate([gathered[256:320, 0:128], gathered[576:640, 0:128]], axis=0)
    )
    wanted = ((lane & 7) == (held & 7)) & (lane < 24)
    occupied = jnp.sum(jnp.where(wanted, pieces, 0.0), axis=1, keepdims=True)
    cells = jnp.zeros((NS, 128), f32)
    for p in range(3):
        mine = slab_of(lax.axis_index("y") + 8 * p) == lax.axis_index("x")
        cells = jnp.where(mine, states[:, p * 128 : p * 128 + 128], cells)
    density = jnp.sum(occupied * (cells * cells), axis=0, keepdims=True) * (1.0 / NS)

    row = lax.broadcasted_iota(jnp.int32, (128, 128), 0)
    col = lax.broadcasted_iota(jnp.int32, (128, 128), 1)
    source = ((row >> 1) & 1) * 64 + (row >> 2) * 2 + (row & 1)
    interleave = jnp.where(col == source, 1.0, 0.0).astype(bf16)
    stacked = jnp.concatenate([own[:, 512:896], own[:, 0:384]], axis=0)
    left = product(interleave, stacked).astype(bf16)
    tiles = lax.dot_general(
        left, states.astype(bf16), (((1,), (1,)), ((), ())), preferred_element_type=f32
    )
    out[:, 0:512] = tiles.astype(bf16)
    high = density.astype(bf16).astype(f32)
    kind = row & 3
    block = jnp.where(kind == 0, high, jnp.where(kind == 1, density - high, 0.0))
    out[:, 512:640] = block.astype(bf16)


def sum_kernel(parts, rows, density):
    row = lax.broadcasted_iota(jnp.int32, (4 * SLABS, 128), 0)
    col = lax.broadcasted_iota(jnp.int32, (4 * SLABS, 128), 1)
    adder = jnp.where((row & 3) == (col & 3), 1.0, 0.0).astype(bf16)
    rows[...] = product(adder, parts[:, 0:512]).astype(bf16)
    row = lax.broadcasted_iota(jnp.int32, (8, 128), 0)
    col = lax.broadcasted_iota(jnp.int32, (8, 128), 1)
    for lane_block in range(4):
        sender = lane_block * 8 + ((THICK * lax.axis_index("x") + row) & 7)
        hit = ((col == sender * 4) | (col == sender * 4 + 1)) & (row < THICK)
        pick = jnp.where(hit, 1.0, 0.0).astype(bf16)
        lanes = slice(lane_block * 128, lane_block * 128 + 128)
        density[:, lanes] = product(pick, parts[:, 512:640])


def final_kernel(received, cells, energy, gram, density):
    rows = received[...].astype(f32)
    scale = 1.0 / (NZ * PLANE)
    for x in range(4):
        total = rows[12 * x : 12 * x + 4] + rows[12 * x + 4 : 12 * x + 8] + rows[12 * x + 8 : 12 * x + 12]
        total = total * scale
        energy[2 * x : 2 * x + 2] = total[0:2]
        gram[2 * x : 2 * x + 2] = total[2:4]
    for line in range(NX):
        density[:, line, :] = cells[0:THICK, line * NY : line * NY + NY]


def exchange(array, axes):
    return lax.all_to_all(array, axes, 0, 0, tiled=True)


def body(orbitals, potential, occupation):
    code = jnp.exp2(CODE * (potential + OFFSET)).astype(bf16)
    wells = jnp.stack([code, code]).reshape(1, 2 * THICK, PLANE)
    rows = jnp.concatenate(
        [orbitals.reshape(4, 2 * THICK, PLANE), jnp.broadcast_to(wells, (4, 2 * THICK, PLANE))], axis=1
    )
    rest = rows[:, 16:18].reshape(4, 8, 128)
    slabs = jnp.concatenate([rows[:, :8], rows[:, 8:16], rest], axis=2)
    slabs = jnp.broadcast_to(slabs[:, None], (4, 3, 8, 1152)).reshape(SLABS, 8, 1152)
    slabs = exchange(slabs, ("x", "zh")).reshape(SLABS * 8, 1152)

    vmem = pl.BlockSpec(memory_space=pltpu.VMEM)
    params = pltpu.CompilerParams(vmem_limit_bytes=24 * 1024 * 1024)
    send = pl.pallas_call(
        filter_kernel,
        out_shape=jax.ShapeDtypeStruct((64, 896), bf16),
        in_specs=[vmem] * 7,
        out_specs=vmem,
        compiler_params=params,
        name="chebyshev",
    )(occupation.reshape(1, 8), slabs, unpack, plane_high, plane_low, depth_high, depth_low)

    own = exchange(send.reshape(32, 2, 896), ("zl", "y")).reshape(64, 896)
    shared = jnp.broadcast_to(own[None, :, :384], (4, 64, 384))
    gathered = exchange(shared, "x").reshape(256, 384)
    gathered, late = lax.optimization_barrier((gathered, own))
    occupied = jnp.pad(late[:, 384:512], ((0, 0), (0, 256)))
    gathered = jnp.concatenate([gathered, occupied], axis=0)
    gathered = lax.all_gather(gathered, "c", axis=0, tiled=True)

    partial = pl.pallas_call(
        tile_kernel,
        out_shape=jax.ShapeDtypeStruct((128, 640), bf16),
        in_specs=[vmem] * 2,
        out_specs=vmem,
        compiler_params=params,
        name="tiles",
    )(own, gathered)

    parts = exchange(partial.reshape(32, 4, 640), ("zl", "y")).reshape(128, 640)
    rows, cells = pl.pallas_call(
        sum_kernel,
        out_shape=[
            jax.ShapeDtypeStruct((4 * SLABS, NS), bf16),
            jax.ShapeDtypeStruct((8, PLANE), f32),
        ],
        in_specs=[vmem],
        out_specs=[vmem] * 2,
        compiler_params=params,
        name="sums",
    )(parts)

    rows = exchange(rows.reshape(SLABS, 4, NS), ("x", "zh")).reshape(4 * SLABS, NS)
    return pl.pallas_call(
        final_kernel,
        out_shape=[
            jax.ShapeDtypeStruct((8, NS), f32),
            jax.ShapeDtypeStruct((8, NS), f32),
            jax.ShapeDtypeStruct((THICK, NX, NY), f32),
        ],
        in_specs=[vmem] * 2,
        out_specs=[vmem] * 3,
        compiler_params=params,
        name="results",
    )(rows, cells)


def solution(mesh):
    fine = Mesh(mesh.devices.reshape(4, 3, 4, 8, 2), ("x", "zh", "zl", "y", "c"))
    grid, state = ("x", "zh"), ("zl", "y", "c")
    return jax.shard_map(
        body,
        mesh=fine,
        in_specs=(P(state, grid, None, None), P(grid, None, None), P(state)),
        out_specs=(P(state, None), P(state, None), P(grid, None, None)),
        check_vma=False,
    )
```

```python
import math

import jax
import jax.numpy as jnp
import numpy as np
from jax import lax
from jax.experimental import pallas as pl
from jax.experimental.pallas import tpu as pltpu
from jax.sharding import Mesh
from jax.sharding import PartitionSpec as P

NS = 512
RADIUS = 6
DEGREE = 4
NX = 16
NY = 32
NZ = 72
PLANE = NX * NY
SLABS = 12
THICK = NZ // SLABS
PICKED = 9 * NZ + 8

stencil_weights = (
    -5369.0 / 1800.0,
    12.0 / 7.0,
    -15.0 / 56.0,
    10.0 / 189.0,
    -1.0 / 112.0,
    2.0 / 1925.0,
    -1.0 / 16632.0,
)
cut_low = 1.0
cut_high = 12.0
centre = 0.5 * (cut_high + cut_low)
spread = 0.5 * (cut_high - cut_low)
CODE = 120.0
OFFSET = 0.5
bf16 = jnp.bfloat16
f32 = jnp.float32


def ring(count):
    line = np.zeros((count, count))
    rows = np.arange(count)
    for reach in range(1, RADIUS + 1):
        line[rows, (rows + reach) % count] += -stencil_weights[reach] / spread
        line[rows, (rows - reach) % count] += -stencil_weights[reach] / spread
    return line


def halves(matrix):
    high = matrix.astype(np.float32).astype(bf16)
    low = (matrix - high.astype(np.float64)).astype(np.float32).astype(bf16)
    return high, low


plane_high, plane_low = halves(
    np.kron(ring(NX), np.eye(NY)) + np.kron(np.eye(NX), ring(NY))
)
depth_high, depth_low = halves(np.kron(np.eye(2), ring(NZ)))


def unpacking():
    matrix = np.zeros((PICKED, SLABS * 8), np.float32)
    for slab in range(SLABS):
        for plane in range(THICK):
            z = slab * THICK + plane
            for state in range(2):
                line = state * THICK + plane
                start = 0 if line < 8 else 6 * NZ
                matrix[start + state * NZ + z, slab * 8 + line % 8] = 1.0
            if plane < 4:
                matrix[8 * NZ + z, slab * 8 + 4 + plane] = 1.0
            else:
                for block in range(4):
                    matrix[(2 + block) * NZ + z, slab * 8 + (plane - 4) * 4 + block] = 1.0
    return matrix.astype(bf16)


unpack = unpacking()


def slab_of(line):
    return sum(jnp.where(line >= THICK * slab, 1, 0) for slab in range(1, 4))


def product(a, b):
    return lax.dot_general(a, b, (((1,), (0,)), ((), ())), preferred_element_type=f32)


def filter_kernel(occupation, slabs, unpack_rows, high_xy, low_xy, high_z, low_z, out):
    count = 2 * NZ
    left, middle, right = slabs[:, 0:512], slabs[:, 512:1024], slabs[:, 1024:1152]
    first = product(unpack_rows[0:count], left) + product(unpack_rows[6 * NZ : 8 * NZ], middle)
    pieces = product(unpack_rows[count : 6 * NZ], right)
    code = product(unpack_rows[8 * NZ : PICKED], middle)[:NZ] + jnp.concatenate(
        [pieces[block * NZ : block * NZ + NZ] for block in range(4)], axis=1
    )
    levels = jnp.log(code) * (1.0 / (CODE * math.log(2.0))) - OFFSET - 1.5 * stencil_weights[0]
    diagonal = jnp.concatenate([levels, levels], axis=0)
    shifted = (diagonal - centre) * (2.0 / spread)

    def hop(v):
        return (
            product(v, high_xy[...])
            + product(v, low_xy[...])
            + product(high_z[...], v)
            + product(low_z[...], v)
        )

    previous = first
    current = ((hop(first.astype(bf16)) + shifted * first) * 0.5).astype(bf16)
    for _ in range(1, DEGREE):
        wide = current.astype(f32)
        following = hop(current) + shifted * wide - previous
        previous = wide
        current = following.astype(bf16)
    applied = (hop(current) * (0.5 * spread) + diagonal * current.astype(f32)).astype(bf16)

    row = lax.broadcasted_iota(jnp.int32, (48, count), 0)
    col = lax.broadcasted_iota(jnp.int32, (48, count), 1)
    line = ((row >> 1) & 7) + 8 * (row >> 4)
    slab = slab_of(line)
    z = THICK * (3 * slab + lax.axis_index("zh")) + line - THICK * slab
    pick = jnp.where(col == (row & 1) * NZ + z, 1.0, 0.0).astype(bf16)
    filtered_rows = product(pick, current).astype(bf16)
    applied_rows = product(pick, applied).astype(bf16)
    for lane_block in range(4):
        lanes = slice(lane_block * 128, lane_block * 128 + 128)
        for p in range(3):
            rows = slice(p * 16, p * 16 + 16)
            target = slice(lane_block * 16, lane_block * 16 + 16)
            out[target, p * 128 : p * 128 + 128] = filtered_rows[rows, lanes]
            out[target, 512 + p * 128 : 640 + p * 128] = applied_rows[rows, lanes]
    lane = lax.broadcasted_iota(jnp.int32, (8, 128), 1)
    held = lax.broadcasted_iota(jnp.int32, (8, 128), 0)
    value = jnp.sum(
        jnp.where(held[:, 0:8] == lane[:, 0:8], occupation[...], 0.0), axis=1, keepdims=True
    )
    block = jnp.zeros((8, 128), f32)
    for piece in range(3):
        part = value.astype(bf16).astype(f32)
        value = value - part
        block = jnp.where(lane == 8 * piece + held, part, block)
    block = jnp.sum(block, axis=0, keepdims=True)
    out[:, 384:512] = jnp.broadcast_to(block, (64, 128)).astype(bf16)


def tile_kernel(own, gathered, out):
    row = lax.broadcasted_iota(jnp.int32, (NS, NS), 0)
    col = lax.broadcasted_iota(jnp.int32, (NS, NS), 1)
    source = ((row >> 3) & 1) * 256 + ((row >> 1) & 3) * 64 + (row >> 4) * 2 + (row & 1)
    order = jnp.where(col == source, 1.0, 0.0).astype(bf16)
    states = product(order, jnp.concatenate([gathered[0:256], gathered[320:576]], axis=0))
    held = lax.broadcasted_iota(jnp.int32, (NS, 128), 0)
    lane = lax.broadcasted_iota(jnp.int32, (NS, 128), 1)
    owner = jnp.where(lane == ((held >> 3) & 1) * 64 + (held >> 4) * 2, 1.0, 0.0).astype(bf16)
    pieces = product(
        owner, jnp.concatenate([gathered[256:320, 0:128], gathered[576:640, 0:128]], axis=0)
    )
    wanted = ((lane & 7) == (held & 7)) & (lane < 24)
    occupied = jnp.sum(jnp.where(wanted, pieces, 0.0), axis=1, keepdims=True)
    cells = jnp.zeros((NS, 128), f32)
    for p in range(3):
        mine = slab_of(lax.axis_index("y") + 8 * p) == lax.axis_index("x")
        cells = jnp.where(mine, states[:, p * 128 : p * 128 + 128], cells)
    density = jnp.sum(occupied * (cells * cells), axis=0, keepdims=True) * (1.0 / NS)

    row = lax.broadcasted_iota(jnp.int32, (128, 128), 0)
    col = lax.broadcasted_iota(jnp.int32, (128, 128), 1)
    source = ((row >> 1) & 1) * 64 + (row >> 2) * 2 + (row & 1)
    interleave = jnp.where(col == source, 1.0, 0.0).astype(bf16)
    stacked = jnp.concatenate([own[:, 512:896], own[:, 0:384]], axis=0)
    left = product(interleave, stacked).astype(bf16)
    tiles = lax.dot_general(
        left, states.astype(bf16), (((1,), (1,)), ((), ())), preferred_element_type=f32
    )
    out[:, 0:512] = tiles.astype(bf16)
    high = density.astype(bf16).astype(f32)
    kind = row & 3
    block = jnp.where(kind == 0, high, jnp.where(kind == 1, density - high, 0.0))
    out[:, 512:640] = block.astype(bf16)


def sum_kernel(parts, rows, density):
    row = lax.broadcasted_iota(jnp.int32, (4 * SLABS, 128), 0)
    col = lax.broadcasted_iota(jnp.int32, (4 * SLABS, 128), 1)
    adder = jnp.where((row & 3) == (col & 3), 1.0, 0.0).astype(bf16)
    rows[...] = product(adder, parts[:, 0:512]).astype(bf16)
    row = lax.broadcasted_iota(jnp.int32, (8, 128), 0)
    col = lax.broadcasted_iota(jnp.int32, (8, 128), 1)
    for lane_block in range(4):
        sender = lane_block * 8 + ((THICK * lax.axis_index("x") + row) & 7)
        hit = ((col == sender * 4) | (col == sender * 4 + 1)) & (row < THICK)
        pick = jnp.where(hit, 1.0, 0.0).astype(bf16)
        lanes = slice(lane_block * 128, lane_block * 128 + 128)
        density[:, lanes] = product(pick, parts[:, 512:640])


def final_kernel(received, cells, energy, gram, density):
    rows = received[...].astype(f32)
    scale = 1.0 / (NZ * PLANE)
    for x in range(4):
        total = rows[12 * x : 12 * x + 4] + rows[12 * x + 4 : 12 * x + 8] + rows[12 * x + 8 : 12 * x + 12]
        total = total * scale
        energy[2 * x : 2 * x + 2] = total[0:2]
        gram[2 * x : 2 * x + 2] = total[2:4]
    for line in range(NX):
        density[:, line, :] = cells[0:THICK, line * NY : line * NY + NY]


def exchange(array, axes):
    return lax.all_to_all(array, axes, 0, 0, tiled=True)


def body(orbitals, potential, occupation):
    code = jnp.exp2(CODE * (potential + OFFSET)).astype(bf16)
    wells = jnp.stack([code, code]).reshape(1, 2 * THICK, PLANE)
    rows = jnp.concatenate(
        [orbitals.reshape(4, 2 * THICK, PLANE), jnp.broadcast_to(wells, (4, 2 * THICK, PLANE))], axis=1
    )
    rest = rows[:, 16:18].reshape(4, 8, 128)
    slabs = jnp.concatenate([rows[:, :8], rows[:, 8:16], rest], axis=2)
    slabs = jnp.broadcast_to(slabs[:, None], (4, 3, 8, 1152)).reshape(SLABS, 8, 1152)
    slabs = exchange(slabs, ("x", "zh")).reshape(SLABS * 8, 1152)

    vmem = pl.BlockSpec(memory_space=pltpu.VMEM)
    params = pltpu.CompilerParams(vmem_limit_bytes=24 * 1024 * 1024)
    send = pl.pallas_call(
        filter_kernel,
        out_shape=jax.ShapeDtypeStruct((64, 896), bf16),
        in_specs=[vmem] * 7,
        out_specs=vmem,
        compiler_params=params,
        name="chebyshev",
    )(occupation.reshape(1, 8), slabs, unpack, plane_high, plane_low, depth_high, depth_low)

    own = exchange(send.reshape(32, 2, 896), ("zl", "y")).reshape(64, 896)
    shared = jnp.broadcast_to(own[None, :, :384], (4, 64, 384))
    gathered = exchange(shared, "x").reshape(256, 384)
    gathered, late = lax.optimization_barrier((gathered, own))
    occupied = jnp.pad(late[:, 384:512], ((0, 0), (0, 256)))
    gathered = jnp.concatenate([gathered, occupied], axis=0)
    gathered = lax.all_gather(gathered, "c", axis=0, tiled=True)

    partial = pl.pallas_call(
        tile_kernel,
        out_shape=jax.ShapeDtypeStruct((128, 640), bf16),
        in_specs=[vmem] * 2,
        out_specs=vmem,
        compiler_params=params,
        name="tiles",
    )(own, gathered)

    parts = exchange(partial.reshape(32, 4, 640), ("zl", "y")).reshape(128, 640)
    rows, cells = pl.pallas_call(
        sum_kernel,
        out_shape=[
            jax.ShapeDtypeStruct((4 * SLABS, NS), bf16),
            jax.ShapeDtypeStruct((8, PLANE), f32),
        ],
        in_specs=[vmem],
        out_specs=[vmem] * 2,
        compiler_params=params,
        name="sums",
    )(parts)

    rows = exchange(rows.reshape(SLABS, 4, NS), ("x", "zh")).reshape(4 * SLABS, NS)
    return pl.pallas_call(
        final_kernel,
        out_shape=[
            jax.ShapeDtypeStruct((8, NS), f32),
            jax.ShapeDtypeStruct((8, NS), f32),
            jax.ShapeDtypeStruct((THICK, NX, NY), f32),
        ],
        in_specs=[vmem] * 2,
        out_specs=[vmem] * 3,
        compiler_params=params,
        name="results",
    )(rows, cells)


def solution(mesh):
    fine = Mesh(mesh.devices.reshape(4, 3, 4, 8, 2), ("x", "zh", "zl", "y", "c"))
    grid, state = ("x", "zh"), ("zl", "y", "c")
    return jax.shard_map(
        body,
        mesh=fine,
        in_specs=(P(state, grid, None, None), P(grid, None, None), P(state)),
        out_specs=(P(state, None), P(state, None), P(grid, None, None)),
        check_vma=False,
    )
```
